256 devices in a mesh: dp: 64 (over z, x, core), replica: 4 (over y).
Axes of the slice: x: 4, y: 4, z: 8, core: 2. Of those that a mesh axis runs over, the one named last changes fastest.
Arguments:
- gradients: bfloat16 [56, 1024, 1024], P(None, 'dp', 'replica')
- adagrad: float32 [56, 1024, 1024], P(None, 'dp', 'replica'), may hold values from 0.003 to 0.03
- factor_left: float32 [128, 1024, 1024], P('dp', 'replica'), may hold values from -4 to 4
- factor_right: float32 [128, 1024, 1024], P('dp', 'replica'), may hold values from -4 to 4
- root_left: bfloat16 [128, 1024, 1024], P('dp', 'replica')
- root_right: bfloat16 [128, 1024, 1024], P('dp', None, 'replica')
- block_slot: int32 [56], replicated, may hold values from 0 to 127, as said below
Outputs:
- update: bfloat16 [56, 1024, 1024], P(None, 'dp', 'replica')
- adagrad_new: float32 [56, 1024, 1024], P(None, 'dp', 'replica')
- factor_left_new: float32 [128, 1024, 1024], P('dp', 'replica')
- factor_right_new: float32 [128, 1024, 1024], P('dp', 'replica')
The draws below stay inside these ranges and needn't reach their ends.
Inputs may be any that keep to these rules, and one draw needn't show every extreme that they name: block_slot holds distinct slot numbers; slot t belongs to owner group t // 2, so an owner group serves 0 to 2 blocks.
All inputs are finite; a program needn't handle non-finite values.
Results may differ from the reference program's by a relative error of at most 0.0058.
Values may be sent and summed in bfloat16 or wider, within the bound.
A program may use at most 64 MiB of HBM per device.

```python
import math
import jax
import jax.numpy as jnp
from jax import lax

B = 1024
TOTAL = 128
NBLK = 56


def draw_gradients(key, part):
    key = jax.random.fold_in(key, 1)
    key_base, key_rows, key_cols = jax.random.split(key, 3)
    row_scale = jnp.exp(jax.random.uniform(key_rows, (NBLK, B, 1), minval=-1.15, maxval=1.15))
    col_scale = jnp.exp(jax.random.uniform(key_cols, (NBLK, 1, B), minval=-1.15, maxval=1.15))
    base = jax.random.normal(key_base, (NBLK, B, B))
    values = 0.1 * base * row_scale * col_scale
    return values.astype(jnp.bfloat16)


def dominant_factor(key):
    key_diag, key_noise = jax.random.split(key)
    diagonal = jnp.exp(jax.random.uniform(key_diag, (TOTAL, B), minval=-0.5, maxval=0.5))
    noise = jax.random.normal(key_noise, (TOTAL, B, B)) * (0.5 / math.sqrt(B))
    identity = (jnp.arange(B)[:, None] == jnp.arange(B)[None, :]).astype(jnp.float32)
    return (identity[None, :, :] * diagonal[:, :, None] + noise).astype(jnp.bfloat16)


def draw_root_left(key, part):
    key = jax.random.fold_in(key, 2)
    return dominant_factor(key)


def draw_root_right(key, part):
    key = jax.random.fold_in(key, 3)
    return dominant_factor(key)


def draw_block_slot(key, part):
    key = jax.random.fold_in(key, 4)
    key_score, key_order = jax.random.split(key)
    score = jax.random.permutation(key_score, TOTAL).astype(jnp.int32)
    slot_ids = jnp.arange(TOTAL, dtype=jnp.int32)
    score = jnp.where(slot_ids == 0, -2, jnp.where(slot_ids == TOTAL - 1, -1, score))
    ordered = jnp.argsort(score, stable=True).astype(jnp.int32)
    chosen = ordered[:NBLK]
    return jax.random.permutation(key_order, chosen).astype(jnp.int32)


def levels(rng, dims, cuts, smallest, largest):
    level = 1.0
    for position, parts in cuts:
        draws = jax.random.uniform(jax.random.fold_in(jax.random.fold_in(rng, 6), position), (parts,), jnp.float32, smallest / len(cuts), largest / len(cuts))
        level = level * jnp.repeat(jnp.exp(draws), dims[position] // parts).reshape((-1,) + (1,) * (len(dims) - 1 - position))
    return level


def gaussian(key, extent, scale, reach, cuts=(), kind=jnp.bfloat16):
    level = levels(key, extent, cuts, -0.22, 0.18) if cuts else 1.0
    drawn = jax.random.normal(key, extent, jnp.float32) * scale * level
    return jnp.minimum(jnp.maximum(drawn, -reach), reach).astype(kind)


def setup_inputs(seed: int = 0) -> dict:
    key_of = jax.random.split(jax.random.key(seed), 8)
    gradients = draw_gradients(jax.random.fold_in(key_of[7], 71), 0)
    adagrad = jnp.clip(jnp.exp(math.log(0.03) - 2.3025851 * jax.random.uniform(key_of[1], (NBLK, B, B), jnp.float32) ** levels(key_of[1], (NBLK, B, B), ((1, 64), (2, 4)), -0.2, 0.2)), 0.003, 0.03)
    factor_left = gaussian(key_of[2], (TOTAL, B, B), 0.3, 4.0, ((0, 64), (1, 4)), jnp.float32)
    factor_right = gaussian(key_of[3], (TOTAL, B, B), 0.3, 4.0, ((0, 64), (1, 4)), jnp.float32)
    root_left = draw_root_left(jax.random.fold_in(key_of[7], 71), 0)
    root_right = draw_root_right(jax.random.fold_in(key_of[7], 71), 0)
    block_slot = draw_block_slot(jax.random.fold_in(key_of[7], 71), 0)
    return {"gradients": gradients, "adagrad": adagrad, "factor_left": factor_left, "factor_right": factor_right, "root_left": root_left, "root_right": root_right, "block_slot": block_slot}


def block_work(operands):
    grad, left, right, root_l, root_r = operands
    left_term = jnp.dot(grad, grad.T, preferred_element_type=jnp.float32)
    right_term = jnp.dot(grad.T, grad, preferred_element_type=jnp.float32)
    half = jnp.dot(root_l, grad, preferred_element_type=jnp.float32).astype(jnp.bfloat16)
    search = jnp.dot(half, root_r, preferred_element_type=jnp.float32).astype(jnp.bfloat16)
    return (0.1 * left_term, 0.1 * right_term, search)

def reference(gradients, adagrad, factor_left, factor_right, root_left, root_right, block_slot):
    index = block_slot.astype(jnp.int32)
    left_terms, right_terms, search = lax.map(block_work, (gradients, factor_left[index], factor_right[index], root_left[index], root_right[index]))
    factor_left_new = (0.9 * factor_left).at[index].add(left_terms)
    factor_right_new = (0.9 * factor_right).at[index].add(right_terms)
    grads32 = gradients.astype(jnp.float32)
    adagrad_new = adagrad + grads32 * grads32
    scaled = grads32 / (jnp.sqrt(adagrad_new) + 1e-08)
    graft_sq = lax.optimization_barrier(jnp.sum(scaled * scaled, axis=(1, 2)))
    search32 = search.astype(jnp.float32)
    search_sq = lax.optimization_barrier(jnp.sum(search32 * search32, axis=(1, 2)))
    ratio = jnp.sqrt(graft_sq) / (jnp.sqrt(search_sq) + 1e-06)
    update = (search32 * ratio[:, None, None]).astype(jnp.bfloat16)
    return (update, adagrad_new, factor_left_new, factor_right_new)
```

```python
import jax
import jax.numpy as jnp
from jax import lax
from jax.experimental import pallas as pl
from jax.experimental.pallas import tpu as pltpu
from jax.sharding import PartitionSpec as P

MESH = pl.DeviceIdType.MESH
NZ, NX, NC, NY = 8, 4, 2, 4
ROWS, COLS, WIDTH = 16, 256, 1024
SLOTS = NZ * NX * NY
NBLK = 56
F32, BF16 = jnp.float32, jnp.bfloat16


def device(z, x, core, y):
    return (z * (NX * NC) + x * NC + core, y)


def drain(ref, sem):
    pltpu.make_async_copy(ref, ref, sem).wait()


def kernel(
    slot_ref, inv_ref, g_ref, a_ref, rl_ref, rr_ref,
    upd_ref, left_ref, right_ref,
    sbuf, gbuf, rlb, rrb, hb, sb, ubr, lb, rb, gp, ar_z, ar_x, ar_y, ar_c,
    g_send, g_recv, gx_send, gx_recv, rl_send, rl_recv, rr_send, rr_recv,
    rx_send, rx_recv, f_send, f_recv, u_send, u_recv,
    z_send, z_recv, x_send, x_recv, y_send, y_recv, c_send, c_recv,
):
    d = lax.axis_index("dp")
    y = lax.axis_index("replica")
    z, x, core = d // (NX * NC), (d // NC) % NX, d % NC
    other = 1 - core
    zx = z * NX + x
    mine = zx * NY + y
    partner = device(z, x, other, y)

    def target(k):
        return (z + k % NZ) % NZ, (x + (k // NZ) % NX) % NX, (y + k // (NZ * NX)) % NY

    def remote(src, dst, send, recv, where):
        return pltpu.make_async_remote_copy(
            src_ref=src, dst_ref=dst, send_sem=send, recv_sem=recv,
            device_id=where, device_id_type=MESH,
        )

    barrier = pltpu.get_barrier_semaphore()

    def greet(k, _):
        tz, tx, ty = target(k)
        pl.semaphore_signal(barrier, inc=1, device_id=device(tz, tx, core, ty), device_id_type=MESH)
        return 0

    lax.fori_loop(1, SLOTS, greet, 0)
    for ty in range(NY):
        pl.semaphore_signal(barrier, inc=1, device_id=device(z, x, other, ty), device_id_type=MESH)

    def pack(t, _):
        b = inv_ref[t]
        rows = g_ref[jnp.minimum(b, NBLK - 1)]
        sbuf[t] = jnp.where(b < NBLK, rows, jnp.zeros_like(rows))
        return 0

    lax.fori_loop(0, SLOTS, pack, 0)
    pl.semaphore_wait(barrier, SLOTS - 1 + NY)

    def send_rows(k, _):
        tz, tx, ty = target(k)
        remote(
            sbuf.at[(tz * NX + tx) * NY + ty], gbuf.at[y, zx, core],
            g_send, g_recv.at[y], device(tz, tx, core, ty),
        ).start()
        return 0

    own_rows = pltpu.make_async_copy(sbuf.at[mine], gbuf.at[y, zx, core], g_recv.at[y])
    own_rows.start()
    lax.fori_loop(1, SLOTS, send_rows, 0)

    half = WIDTH // 2

    def root_parts(i, q):
        return (
            (rl_ref.at[i, :, q], rlb.at[pl.ds(y * 8, 8)], rl_send.at[i, q], rl_recv),
            (rr_ref.at[i, pl.ds(q * half, half)], rrb.at[y, pl.ds(q * half, half)], rr_send.at[i, q], rr_recv),
        )

    def is_self(i, q):
        return jnp.logical_and(2 * core + i == y, core == q)

    for i in range(2):
        for q in range(NC):
            for src, dst, send, recv in root_parts(i, q):
                @pl.when(is_self(i, q))
                def _(src=src, dst=dst, recv=recv):
                    pltpu.make_async_copy(src, dst, recv).start()

                @pl.when(jnp.logical_not(is_self(i, q)))
                def _(src=src, dst=dst, send=send, recv=recv, i=i, q=q):
                    remote(src, dst, send, recv, device(z, x, q, 2 * core + i)).start()

    gp[...] = jnp.zeros_like(gp)

    def graft(b, _):
        g32 = g_ref[b].astype(F32)
        scaled = g32 / (jnp.sqrt(a_ref[b] + g32 * g32) + 1e-08)
        sq = jnp.sum(scaled * scaled, axis=0, keepdims=True)
        gp[pl.ds(b, 1), :] = sq[:, :128] + sq[:, 128:]
        return 0

    lax.fori_loop(0, NBLK, graft, 0)
    part = jnp.sum(jnp.transpose(gp[...]), axis=0, keepdims=True)
    ar_z[z] = jnp.broadcast_to(part, (8, 128))

    def spread(buf, me, count, send, recv, where):
        copies = []
        for k in range(1, count):
            other_one = (me + k) % count
            copies.append(remote(buf.at[me], buf.at[me], send.at[k], recv.at[k], where(other_one)))
        for cp in copies:
            cp.start()
        return copies

    z_copies = spread(ar_z, z, NZ, z_send, z_recv, lambda o: device(o, x, core, y))

    swaps = []
    for c in range(NY):
        drain(gbuf.at[c, :, core], g_recv.at[c])
        cp = remote(gbuf.at[c, :, core], gbuf.at[c, :, core], gx_send.at[c], gx_recv.at[c], partner)
        cp.start()
        swaps.append(cp)
    for cp in z_copies:
        cp.wait()
    ar_x[x] = jnp.sum(ar_z[...], axis=0)
    x_copies = spread(ar_x, x, NX, x_send, x_recv, lambda o: device(z, o, core, y))
    for cp in swaps:
        cp.wait_recv()

    owner = y // 2
    i_mine = y % 2

    def factor_part(n):
        r = 2 * core + n
        acc = jnp.zeros((COLS, WIDTH), F32)
        for c in range(NY):
            rows = gbuf[c, pl.ds(r * 8, 8)].reshape(COLS, COLS)
            acc = acc + lax.dot_general(
                rows, gbuf[c].reshape(WIDTH, COLS), (((1,), (1,)), ((), ())), preferred_element_type=F32
            )
        lb[n] = acc.astype(BF16)
        cols = gbuf[r].reshape(WIDTH, COLS)
        for c in range(NY):
            rb[n, :, c * COLS:(c + 1) * COLS] = lax.dot_general(
                cols, gbuf[c].reshape(WIDTH, COLS), (((0,), (0,)), ((), ())), preferred_element_type=F32
            ).astype(BF16)

    def factor_self(n):
        return jnp.logical_and(2 * core + n == y, core == owner)

    for n in range(2):
        factor_part(n)
        for m, (src, dst) in enumerate(((lb.at[n], left_ref.at[i_mine]), (rb.at[n], right_ref.at[i_mine]))):
            @pl.when(factor_self(n))
            def _(src=src, dst=dst, m=m):
                pltpu.make_async_copy(src, dst, f_recv.at[m]).start()

            @pl.when(jnp.logical_not(factor_self(n)))
            def _(src=src, dst=dst, m=m, n=n):
                remote(src, dst, f_send.at[n, m], f_recv.at[m], device(z, x, owner, 2 * core + n)).start()

    for cp in x_copies:
        cp.wait()
    ar_y[y] = jnp.sum(ar_x[...], axis=0)
    y_copies = spread(ar_y, y, NY, y_send, y_recv, lambda o: device(z, x, core, o))

    drain(rrb.at[:, pl.ds(core * half, half)], rr_recv)
    rr_swap = remote(
        rrb.at[:, pl.ds(core * half, half)], rrb.at[:, pl.ds(core * half, half)], rx_send, rx_recv, partner
    )
    rr_swap.start()
    drain(rlb, rl_recv)
    rl = rlb[...].reshape(half, WIDTH)
    for c in range(NY):
        hb[:, c * COLS:(c + 1) * COLS] = jnp.dot(
            rl, gbuf[c].reshape(WIDTH, COLS), preferred_element_type=F32
        ).astype(BF16)
    rr_swap.wait_recv()
    sq = jnp.zeros((8, 128), F32)
    for c in range(NY):
        s = jnp.dot(hb[...], rrb[c], preferred_element_type=F32).astype(BF16)
        sb[c] = s.reshape(NZ * NX, ROWS, COLS)
        s32 = s.astype(F32)
        s2 = jnp.sum((s32 * s32).reshape(half // 8, 8, COLS), axis=0)
        sq = sq + s2[:, :128] + s2[:, 128:]
    for cp in y_copies:
        cp.wait()
    ar_c[core, 0] = sq
    ar_c[core, 1] = jnp.sum(ar_y[...], axis=0)
    c_copy = remote(ar_c.at[core], ar_c.at[core], c_send, c_recv, partner)
    c_copy.start()
    c_copy.wait()
    search_sq = jnp.sum(ar_c[0, 0] + ar_c[1, 0], keepdims=True)
    graft_all = ar_c[0, 1, 0:1] + ar_c[1, 1, 0:1]
    lane = lax.broadcasted_iota(jnp.int32, (1, 128), 1)
    graft_sq = jnp.sum(jnp.where(lane == inv_ref[mine], graft_all, 0.0), keepdims=True)
    ratio = jnp.sqrt(graft_sq) / (jnp.sqrt(search_sq) + 1e-06)
    ratio = jnp.broadcast_to(ratio, (1, COLS))

    def scale(k, _):
        for c in range(NY):
            sb[c, k] = (sb[c, k].astype(F32) * ratio).astype(BF16)
        return 0

    lax.fori_loop(0, NZ * NX, scale, 0)

    own_dir = pltpu.make_async_copy(sb.at[y, zx], ubr.at[mine], u_recv)
    own_dir.start()

    def send_dir(k, _):
        tz, tx, ty = target(k)
        remote(
            sb.at[ty, tz * NX + tx], ubr.at[mine], u_send, u_recv, device(tz, tx, core, ty)
        ).start()
        return 0

    lax.fori_loop(1, SLOTS, send_dir, 0)

    drain(ubr, u_recv)

    def pick(b, _):
        upd_ref[b] = ubr[slot_ref[b]]
        return 0

    lax.fori_loop(0, NBLK, pick, 0)

    drain(left_ref, f_recv.at[0])
    drain(right_ref, f_recv.at[1])
    drain(sbuf.at[pl.ds(0, SLOTS - 1)], g_send)
    drain(ubr.at[pl.ds(0, SLOTS - 1)], u_send)
    for cp in swaps:
        cp.wait_send()
    rr_swap.wait_send()
    for i in range(2):
        for q in range(NC):
            @pl.when(jnp.logical_not(is_self(i, q)))
            def _(i=i, q=q):
                for src, dst, send, recv in root_parts(i, q):
                    drain(dst, send)
    for n in range(2):
        @pl.when(jnp.logical_not(factor_self(n)))
        def _(n=n):
            drain(lb.at[n], f_send.at[n, 0])
            drain(rb.at[n], f_send.at[n, 1])


def exchange(block_slot, inverse, gradients, adagrad, root_left, root_right):
    vmem = pl.BlockSpec(memory_space=pltpu.VMEM)
    smem = pl.BlockSpec(memory_space=pltpu.SMEM)
    hbm = pl.BlockSpec(memory_space=pl.ANY)
    dma = pltpu.SemaphoreType.DMA
    return pl.pallas_call(
        kernel,
        out_shape=(
            jax.ShapeDtypeStruct((NBLK, ROWS, COLS), BF16),
            jax.ShapeDtypeStruct((2, COLS, WIDTH), BF16),
            jax.ShapeDtypeStruct((2, COLS, WIDTH), BF16),
        ),
        in_specs=[smem, smem, vmem, vmem, hbm, hbm],
        out_specs=(vmem, hbm, hbm),
        scratch_shapes=[
            pltpu.VMEM((SLOTS, ROWS, COLS), BF16),
            pltpu.VMEM((NY, NZ * NX, NC, ROWS, COLS), BF16),
            pltpu.VMEM((NZ * NX, ROWS, WIDTH), BF16),
            pltpu.VMEM((NY, WIDTH, COLS), BF16),
            pltpu.VMEM((WIDTH // 2, WIDTH), BF16),
            pltpu.VMEM((NY, NZ * NX, ROWS, COLS), BF16),
            pltpu.VMEM((SLOTS, ROWS, COLS), BF16),
            pltpu.VMEM((2, COLS, WIDTH), BF16),
            pltpu.VMEM((2, COLS, WIDTH), BF16),
            pltpu.VMEM((128, 128), F32),
            pltpu.VMEM((NZ, 8, 128), F32),
            pltpu.VMEM((NX, 8, 128), F32),
            pltpu.VMEM((NY, 8, 128), F32),
            pltpu.VMEM((NC, 2, 8, 128), F32),
            dma, dma((NY,)), dma((NY,)), dma((NY,)), dma((2, NC)), dma, dma((2, NC)), dma,
            dma, dma, dma((2, 2)), dma((2,)), dma, dma,
            dma((NZ,)), dma((NZ,)), dma((NX,)), dma((NX,)), dma((NY,)), dma((NY,)), dma, dma,
        ],
        compiler_params=pltpu.CompilerParams(
            collective_id=0, has_side_effects=True, vmem_limit_bytes=48 * 2**20
        ),
        name="shampoo_exchange",
    )(block_slot, inverse, gradients, adagrad, root_left, root_right)


def on_device(gradients, adagrad, factor_left, factor_right, root_left, root_right, block_slot):
    count = factor_left.shape[0]
    numbers = jnp.arange(NBLK, dtype=jnp.int32)
    named = jnp.arange(SLOTS, dtype=jnp.int32)[:, None] == block_slot[None, :]
    inverse = jnp.min(jnp.where(named, numbers[None, :], NBLK), axis=1)
    update, left_term, right_term = exchange(
        block_slot, inverse, gradients, adagrad,
        root_left.reshape(count, 8, NC, ROWS, WIDTH), root_right,
    )
    grads32 = gradients.astype(F32)
    adagrad_new = adagrad + grads32 * grads32
    factor_left_new = 0.9 * factor_left + 0.1 * left_term.astype(F32)
    factor_right_new = 0.9 * factor_right + 0.1 * right_term.astype(F32)
    return update, adagrad_new, factor_left_new, factor_right_new


def solution(mesh):
    placed = (
        P(None, "dp", "replica"),
        P(None, "dp", "replica"),
        P("dp", "replica", None),
        P("dp", "replica", None),
        P("dp", "replica", None),
        P("dp", None, "replica"),
        P(),
    )
    return jax.shard_map(
        on_device,
        mesh=mesh,
        in_specs=placed,
        out_specs=(
            P(None, "dp", "replica"),
            P(None, "dp", "replica"),
            P("dp", "replica", None),
            P("dp", "replica", None),
        ),
        check_vma=False,
    )
```

```python
import jax
import jax.numpy as jnp
from jax import lax
from jax.experimental import pallas as pl
from jax.experimental.pallas import tpu as pltpu
from jax.sharding import PartitionSpec as P

MESH = pl.DeviceIdType.MESH
NZ, NX, NC, NY = 8, 4, 2, 4
ROWS, COLS, WIDTH = 16, 256, 1024
SLOTS = NZ * NX * NY
NBLK = 56
F32, BF16 = jnp.float32, jnp.bfloat16


def device(z, x, core, y):
    return (z * (NX * NC) + x * NC + core, y)


def drain(ref, sem):
    pltpu.make_async_copy(ref, ref, sem).wait()


def kernel(
    slot_ref, inv_ref, g_hbm, a_hbm, rl_ref, rr_ref,
    upd_ref, left_ref, right_ref,
    g_ref, a_ref, in_sem, meet, sbuf, gbuf, rlb, rrb, hb, sb, ubr, lb, rb, gp, ar_z, ar_x, ar_y, ar_c,
    g_send, g_recv, gx_send, gx_recv, root_send, root_recv,
    rx_send, rx_recv, f_send, f_recv, u_send, u_recv,
    z_send, z_recv, x_send, x_recv, y_send, y_recv, c_send, c_recv,
):
    d = lax.axis_index("dp")
    y = lax.axis_index("replica")
    z, x, core = d // (NX * NC), (d // NC) % NX, d % NC
    other = 1 - core
    zx = z * NX + x
    mine = zx * NY + y
    partner = device(z, x, other, y)

    def target(k):
        m = (k * 37) % SLOTS
        return (z + m % NZ) % NZ, (x + (m // NZ) % NX) % NX, (y + m // (NZ * NX)) % NY

    def remote(src, dst, send, recv, where):
        return pltpu.make_async_remote_copy(
            src_ref=src, dst_ref=dst, send_sem=send, recv_sem=recv,
            device_id=where, device_id_type=MESH,
        )

    loads = [
        pltpu.make_async_copy(g_hbm, g_ref, in_sem.at[0]),
        pltpu.make_async_copy(a_hbm, a_ref, in_sem.at[1]),
    ]
    for cp in loads:
        cp.start()

    along_z = [device((z + k) % NZ, x, core, y) for k in range(1, NZ)]
    along_x = [device(z, (x + k) % NX, core, y) for k in range(1, NX)]
    along_y = [device(z, x, core, (y + k) % NY) for k in range(1, NY)]
    barrier = pltpu.get_barrier_semaphore()

    def greet(sem, devices):
        for one in devices:
            pl.semaphore_signal(sem, inc=1, device_id=one, device_id_type=MESH)

    first = along_z + along_x + along_y + [partner]
    greet(barrier, first)

    def pack(t, _):
        b = inv_ref[t]
        rows = g_ref[jnp.minimum(b, NBLK - 1)]
        sbuf[t] = jnp.where(b < NBLK, rows, jnp.zeros_like(rows))
        return 0

    loads[0].wait()
    lax.fori_loop(0, SLOTS, pack, 0)
    pl.semaphore_wait(barrier, len(first))
    greet(meet.at[0], along_y)
    pl.semaphore_wait(meet.at[0], len(along_y))
    greet(meet.at[1], along_x)
    pl.semaphore_wait(meet.at[1], len(along_x))

    half = WIDTH // 2
    own_rows = pltpu.make_async_copy(sbuf.at[mine], gbuf.at[y, zx, core], g_recv.at[y])
    own_rows.start()

    def send_rows(k):
        tz, tx, ty = target(k)
        remote(
            sbuf.at[(tz * NX + tx) * NY + ty], gbuf.at[y, zx, core],
            g_send, g_recv.at[y], device(tz, tx, core, ty),
        ).start()

    def is_self(i, q):
        return jnp.logical_and(2 * core + i == y, core == q)

    def send_root(i, q, m, n):
        if m == 0:
            src, dst = rl_ref.at[i, n, q], rlb.at[y * 8 + n]
        else:
            rows = pl.ds(pl.multiple_of(q * half + n * (half // 8), half // 8), half // 8)
            src, dst = rr_ref.at[i, rows], rrb.at[y, rows]

        @pl.when(is_self(i, q))
        def _():
            pltpu.make_async_copy(src, dst, root_recv.at[m]).start()

        @pl.when(jnp.logical_not(is_self(i, q)))
        def _():
            remote(src, dst, root_send.at[m, i, q], root_recv.at[m], device(z, x, q, 2 * core + i)).start()

    def send_all(n, _):
        for u, (i, q, m) in enumerate([(i, q, m) for i in range(2) for q in range(NC) for m in range(2)]):
            @pl.when(n * 16 + 2 * u > 0)
            def _(u=u):
                send_rows(n * 16 + 2 * u)

            send_root(i, q, m, n)
            send_rows(n * 16 + 2 * u + 1)
        return 0

    lax.fori_loop(0, 8, send_all, 0)

    gp[...] = jnp.zeros_like(gp)

    def graft(b, _):
        g32 = g_ref[b].astype(F32)
        scaled = g32 / (jnp.sqrt(a_ref[b] + g32 * g32) + 1e-08)
        sq = jnp.sum(scaled * scaled, axis=0, keepdims=True)
        gp[pl.ds(b, 1), :] = sq[:, :128] + sq[:, 128:]
        return 0

    loads[1].wait()
    lax.fori_loop(0, NBLK, graft, 0)
    part = jnp.sum(jnp.transpose(gp[...]), axis=0, keepdims=True)
    ar_z[z] = jnp.broadcast_to(part, (8, 128))

    def spread(buf, me, count, send, recv, where):
        copies = []
        for k in range(1, count):
            other_one = (me + k) % count
            copies.append(remote(buf.at[me], buf.at[me], send.at[k], recv.at[k], where(other_one)))
        for cp in copies:
            cp.start()
        return copies

    z_copies = spread(ar_z, z, NZ, z_send, z_recv, lambda o: device(o, x, core, y))

    swaps = []
    for c in range(NY):
        drain(gbuf.at[c, :, core], g_recv.at[c])
        cp = remote(gbuf.at[c, :, core], gbuf.at[c, :, core], gx_send.at[c], gx_recv.at[c], partner)
        cp.start()
        swaps.append(cp)
    for cp in z_copies:
        cp.wait()
    ar_x[x] = jnp.sum(ar_z[...], axis=0)
    x_copies = spread(ar_x, x, NX, x_send, x_recv, lambda o: device(z, o, core, y))
    for cp in swaps:
        cp.wait_recv()

    owner = y // 2
    i_mine = y % 2

    def left_part(n):
        r = 2 * core + n
        acc = jnp.zeros((COLS, WIDTH), F32)
        for c in range(NY):
            rows = gbuf[c, pl.ds(r * 8, 8)].reshape(COLS, COLS)
            acc = acc + lax.dot_general(
                rows, gbuf[c].reshape(WIDTH, COLS), (((1,), (1,)), ((), ())), preferred_element_type=F32
            )
        lb[n] = acc.astype(BF16).reshape(ROWS, ROWS, WIDTH)

    def right_part(n):
        cols = gbuf[2 * core + n].reshape(WIDTH, COLS)
        for c in range(NY):
            rb[n, :, :, c * COLS:(c + 1) * COLS] = lax.dot_general(
                cols, gbuf[c].reshape(WIDTH, COLS), (((0,), (0,)), ((), ())), preferred_element_type=F32
            ).astype(BF16).reshape(ROWS, ROWS, COLS)

    def factor_self(n):
        return jnp.logical_and(2 * core + n == y, core == owner)

    def send_factor(m, n, piece):
        src = (lb, rb)[m].at[n, piece]
        dst = (left_ref, right_ref)[m].at[i_mine, piece]

        @pl.when(factor_self(n))
        def _():
            pltpu.make_async_copy(src, dst, f_recv.at[m]).start()

        @pl.when(jnp.logical_not(factor_self(n)))
        def _():
            remote(src, dst, f_send.at[m, n], f_recv.at[m], device(z, x, owner, 2 * core + n)).start()

    def send_left(piece, _):
        for n in range(2):
            send_factor(0, n, piece)
        return 0

    for n in range(2):
        left_part(n)
    lax.fori_loop(0, ROWS, send_left, 0)
    for n in range(2):
        right_part(n)

    for cp in x_copies:
        cp.wait()
    ar_y[y] = jnp.sum(ar_x[...], axis=0)
    y_copies = spread(ar_y, y, NY, y_send, y_recv, lambda o: device(z, x, core, o))

    drain(rrb.at[:, pl.ds(core * half, half)], root_recv.at[1])
    rr_swap = remote(
        rrb.at[:, pl.ds(core * half, half)], rrb.at[:, pl.ds(core * half, half)], rx_send, rx_recv, partner
    )
    rr_swap.start()
    drain(rlb, root_recv.at[0])
    rl = rlb[...].reshape(half, WIDTH)
    for c in range(NY):
        hb[:, c * COLS:(c + 1) * COLS] = jnp.dot(
            rl, gbuf[c].reshape(WIDTH, COLS), preferred_element_type=F32
        ).astype(BF16)
    rr_swap.wait_recv()
    sq = jnp.zeros((8, 128), F32)
    for c in range(NY):
        s = jnp.dot(hb[...], rrb[c], preferred_element_type=F32).astype(BF16)
        sb[c] = s.reshape(NZ * NX, ROWS, COLS)
        s32 = s.astype(F32)
        s2 = jnp.sum((s32 * s32).reshape(half // 8, 8, COLS), axis=0)
        sq = sq + s2[:, :128] + s2[:, 128:]
    for cp in y_copies:
        cp.wait()
    ar_c[core, 0] = sq
    ar_c[core, 1] = jnp.sum(ar_y[...], axis=0)
    c_copy = remote(ar_c.at[core], ar_c.at[core], c_send, c_recv, partner)
    c_copy.start()
    c_copy.wait()
    search_sq = jnp.sum(ar_c[0, 0] + ar_c[1, 0], keepdims=True)
    graft_all = ar_c[0, 1, 0:1] + ar_c[1, 1, 0:1]
    lane = lax.broadcasted_iota(jnp.int32, (1, 128), 1)
    graft_sq = jnp.sum(jnp.where(lane == inv_ref[mine], graft_all, 0.0), keepdims=True)
    ratio = jnp.sqrt(graft_sq) / (jnp.sqrt(search_sq) + 1e-06)
    ratio = jnp.broadcast_to(ratio, (1, COLS))

    def scale(k, _):
        for c in range(NY):
            sb[c, k] = (sb[c, k].astype(F32) * ratio).astype(BF16)
        return 0

    lax.fori_loop(0, NZ * NX, scale, 0)

    own_dir = pltpu.make_async_copy(sb.at[y, zx], ubr.at[mine], u_recv)
    own_dir.start()

    def send_dir(k):
        tz, tx, ty = target(k)
        remote(
            sb.at[ty, tz * NX + tx], ubr.at[mine], u_send, u_recv, device(tz, tx, core, ty)
        ).start()

    def send_back(n, _):
        for u in range(8):
            @pl.when(n * 8 + u > 0)
            def _(u=u):
                send_dir(n * 8 + u)

            if u % 4 == 3:
                send_factor(1, u // 4, n)
        return 0

    lax.fori_loop(0, ROWS, send_back, 0)

    drain(ubr, u_recv)

    def pick(b, _):
        upd_ref[b] = ubr[slot_ref[b]]
        return 0

    lax.fori_loop(0, NBLK, pick, 0)

    drain(left_ref, f_recv.at[0])
    drain(right_ref, f_recv.at[1])
    drain(sbuf.at[pl.ds(0, SLOTS - 1)], g_send)
    drain(ubr.at[pl.ds(0, SLOTS - 1)], u_send)
    for cp in swaps:
        cp.wait_send()
    rr_swap.wait_send()
    for i in range(2):
        for q in range(NC):
            @pl.when(jnp.logical_not(is_self(i, q)))
            def _(i=i, q=q):
                drain(rlb.at[pl.ds(0, 8)], root_send.at[0, i, q])
                drain(rrb.at[0, pl.ds(0, half)], root_send.at[1, i, q])
    for n in range(2):
        @pl.when(jnp.logical_not(factor_self(n)))
        def _(n=n):
            drain(lb.at[n], f_send.at[0, n])
            drain(rb.at[n], f_send.at[1, n])


def exchange(block_slot, inverse, gradients, adagrad, root_left, root_right):
    vmem = pl.BlockSpec(memory_space=pltpu.VMEM)
    smem = pl.BlockSpec(memory_space=pltpu.SMEM)
    hbm = pl.BlockSpec(memory_space=pl.ANY)
    dma = pltpu.SemaphoreType.DMA
    return pl.pallas_call(
        kernel,
        out_shape=(
            jax.ShapeDtypeStruct((NBLK, ROWS, COLS), BF16),
            jax.ShapeDtypeStruct((2, ROWS, ROWS, WIDTH), BF16),
            jax.ShapeDtypeStruct((2, ROWS, ROWS, WIDTH), BF16),
        ),
        in_specs=[smem, smem, hbm, hbm, hbm, hbm],
        out_specs=(vmem, hbm, hbm),
        scratch_shapes=[
            pltpu.VMEM((NBLK, ROWS, COLS), BF16),
            pltpu.VMEM((NBLK, ROWS, COLS), F32),
            dma((2,)),
            pltpu.SemaphoreType.REGULAR((2,)),
            pltpu.VMEM((SLOTS, ROWS, COLS), BF16),
            pltpu.VMEM((NY, NZ * NX, NC, ROWS, COLS), BF16),
            pltpu.VMEM((NZ * NX, ROWS, WIDTH), BF16),
            pltpu.VMEM((NY, WIDTH, COLS), BF16),
            pltpu.VMEM((WIDTH // 2, WIDTH), BF16),
            pltpu.VMEM((NY, NZ * NX, ROWS, COLS), BF16),
            pltpu.VMEM((SLOTS, ROWS, COLS), BF16),
            pltpu.VMEM((2, ROWS, ROWS, WIDTH), BF16),
            pltpu.VMEM((2, ROWS, ROWS, WIDTH), BF16),
            pltpu.VMEM((128, 128), F32),
            pltpu.VMEM((NZ, 8, 128), F32),
            pltpu.VMEM((NX, 8, 128), F32),
            pltpu.VMEM((NY, 8, 128), F32),
            pltpu.VMEM((NC, 2, 8, 128), F32),
            dma, dma((NY,)), dma((NY,)), dma((NY,)), dma((2, 2, NC)), dma((2,)),
            dma, dma, dma((2, 2)), dma((2,)), dma, dma,
            dma((NZ,)), dma((NZ,)), dma((NX,)), dma((NX,)), dma((NY,)), dma((NY,)), dma, dma,
        ],
        compiler_params=pltpu.CompilerParams(
            collective_id=0, has_side_effects=True, vmem_limit_bytes=56 * 2**20
        ),
        name="shampoo_exchange",
    )(block_slot, inverse, gradients, adagrad, root_left, root_right)


def on_device(gradients, adagrad, factor_left, factor_right, root_left, root_right, block_slot):
    count = factor_left.shape[0]
    numbers = jnp.arange(NBLK, dtype=jnp.int32)
    named = jnp.arange(SLOTS, dtype=jnp.int32)[:, None] == block_slot[None, :]
    inverse = jnp.min(jnp.where(named, numbers[None, :], NBLK), axis=1)
    update, left_term, right_term = exchange(
        block_slot, inverse, gradients, adagrad,
        root_left.reshape(count, 8, NC, ROWS, WIDTH), root_right,
    )
    grads32 = gradients.astype(F32)
    adagrad_new = adagrad + grads32 * grads32
    factor_left_new = 0.9 * factor_left + 0.1 * left_term.reshape(factor_left.shape).astype(F32)
    factor_right_new = 0.9 * factor_right + 0.1 * right_term.reshape(factor_right.shape).astype(F32)
    return update, adagrad_new, factor_left_new, factor_right_new


def solution(mesh):
    placed = (
        P(None, "dp", "replica"),
        P(None, "dp", "replica"),
        P("dp", "replica", None),
        P("dp", "replica", None),
        P("dp", "replica", None),
        P("dp", None, "replica"),
        P(),
    )
    return jax.shard_map(
        on_device,
        mesh=mesh,
        in_specs=placed,
        out_specs=(
            P(None, "dp", "replica"),
            P(None, "dp", "replica"),
            P("dp", "replica", None),
            P("dp", "replica", None),
        ),
        check_vma=False,
    )
```

```python
import jax
import jax.numpy as jnp
from jax import lax
from jax.experimental import pallas as pl
from jax.experimental.pallas import tpu as pltpu
from jax.sharding import PartitionSpec as P

MESH = pl.DeviceIdType.MESH
NZ, NX, NC, NY = 8, 4, 2, 4
ROWS, COLS, WIDTH = 16, 256, 1024
SLOTS = NZ * NX * NY
NBLK = 56
F32, BF16 = jnp.float32, jnp.bfloat16


def device(z, x, core, y):
    return (z * (NX * NC) + x * NC + core, y)


def in_hbm(value):
    return pltpu.with_memory_space_constraint(value, pltpu.HBM)


def drain(ref, sem):
    pltpu.make_async_copy(ref, ref, sem).wait()


def kernel(
    slot_row, g_hbm, a_hbm, rl_ref, rr_ref,
    ubr, left_ref, right_ref,
    g_ref, a_ref, in_sem, meet, inv_v, inv_ref, sbuf, gbuf, rlb, rrb, hb, sb, lb, rb, gp, ar_z, ar_x, ar_y, ar_c,
    g_send, g_recv, gx_send, gx_recv, root_send, root_recv,
    rx_send, rx_recv, f_send, f_recv, u_send, u_recv,
    z_send, z_recv, x_send, x_recv, y_send, y_recv, c_send, c_recv,
):
    d = lax.axis_index("dp")
    y = lax.axis_index("replica")
    z, x, core = d // (NX * NC), (d // NC) % NX, d % NC
    other = 1 - core
    zx = z * NX + x
    mine = zx * NY + y
    partner = device(z, x, other, y)

    def target(k):
        m = (k * 37) % SLOTS
        return (z + m % NZ) % NZ, (x + (m // NZ) % NX) % NX, (y + m // (NZ * NX)) % NY

    def remote(src, dst, send, recv, where):
        return pltpu.make_async_remote_copy(
            src_ref=src, dst_ref=dst, send_sem=send, recv_sem=recv,
            device_id=where, device_id_type=MESH,
        )

    loads = [
        pltpu.make_async_copy(g_hbm, g_ref, in_sem.at[0]),
        pltpu.make_async_copy(a_hbm, a_ref, in_sem.at[1]),
    ]
    for cp in loads:
        cp.start()

    along_z = [device((z + k) % NZ, x, core, y) for k in range(1, NZ)]
    along_x = [device(z, (x + k) % NX, core, y) for k in range(1, NX)]
    along_y = [device(z, x, core, (y + k) % NY) for k in range(1, NY)]
    barrier = pltpu.get_barrier_semaphore()

    def greet(sem, devices):
        for one in devices:
            pl.semaphore_signal(sem, inc=1, device_id=one, device_id_type=MESH)

    first = along_z + along_x + along_y + [partner]
    greet(barrier, first)

    at_slot = lax.broadcasted_iota(jnp.int32, (SLOTS, NBLK), 0) == slot_row[...]
    block = lax.broadcasted_iota(jnp.int32, (SLOTS, NBLK), 1)
    block = jnp.min(jnp.where(at_slot, block, NBLK), axis=1, keepdims=True)
    inv_v[...] = jnp.transpose(jnp.broadcast_to(block, (SLOTS, 128)))[:8]
    to_smem = pltpu.make_async_copy(inv_v, inv_ref, in_sem.at[2])
    to_smem.start()
    to_smem.wait()

    def pack(t, _):
        b = inv_ref[0, t]
        rows = g_ref[jnp.clip(b, 0, NBLK - 1)]
        sbuf[t] = jnp.where(b < NBLK, rows, jnp.zeros_like(rows))
        return 0

    loads[0].wait()
    lax.fori_loop(0, SLOTS, pack, 0)
    pl.semaphore_wait(barrier, len(first))
    greet(meet.at[0], along_y)
    pl.semaphore_wait(meet.at[0], len(along_y))
    greet(meet.at[1], along_x)
    pl.semaphore_wait(meet.at[1], len(along_x))

    half = WIDTH // 2
    own_rows = pltpu.make_async_copy(sbuf.at[mine], gbuf.at[y, zx, core], g_recv.at[y])
    own_rows.start()

    def send_rows(k):
        tz, tx, ty = target(k)
        remote(
            sbuf.at[(tz * NX + tx) * NY + ty], gbuf.at[y, zx, core],
            g_send, g_recv.at[y], device(tz, tx, core, ty),
        ).start()

    def is_self(i, q):
        return jnp.logical_and(2 * core + i == y, core == q)

    def send_root(i, q, m, n):
        if m == 0:
            src, dst = rl_ref.at[i, n, q], rlb.at[y * 8 + n]
        else:
            rows = pl.ds(pl.multiple_of(q * half + n * (half // 8), half // 8), half // 8)
            src, dst = rr_ref.at[i, rows], rrb.at[y, rows]

        @pl.when(is_self(i, q))
        def _():
            pltpu.make_async_copy(src, dst, root_recv.at[m]).start()

        @pl.when(jnp.logical_not(is_self(i, q)))
        def _():
            remote(src, dst, root_send.at[m, i, q], root_recv.at[m], device(z, x, q, 2 * core + i)).start()

    def send_first(n, _):
        for u in range(16):
            @pl.when(n * 16 + u > 0)
            def _(u=u):
                send_rows(n * 16 + u)
        return 0

    def send_roots(n, _):
        for i, q, m in [(i, q, m) for i in range(2) for q in range(NC) for m in range(2)]:
            send_root(i, q, m, n)
        return 0

    lax.fori_loop(0, 8, send_first, 0)
    lax.fori_loop(0, 1, send_roots, 0)

    gp[...] = jnp.zeros_like(gp)

    def graft(b, _):
        g32 = g_ref[b].astype(F32)
        scaled = g32 / (jnp.sqrt(a_ref[b] + g32 * g32) + 1e-08)
        sq = jnp.sum(scaled * scaled, axis=0, keepdims=True)
        gp[pl.ds(b, 1), :] = sq[:, :128] + sq[:, 128:]
        return 0

    loads[1].wait()
    lax.fori_loop(0, NBLK, graft, 0)
    part = jnp.sum(jnp.transpose(gp[...]), axis=0, keepdims=True)
    ar_y[y] = jnp.broadcast_to(part, (8, 128))

    def spread(buf, me, count, send, recv, where):
        copies = []
        for k in range(1, count):
            other_one = (me + k) % count
            copies.append(remote(buf.at[me], buf.at[me], send.at[k], recv.at[k], where(other_one)))
        for cp in copies:
            cp.start()
        return copies

    y_copies = spread(ar_y, y, NY, y_send, y_recv, lambda o: device(z, x, core, o))
    lax.fori_loop(1, 8, send_roots, 0)
    for cp in y_copies:
        cp.wait()
    ar_x[x] = jnp.sum(ar_y[...], axis=0)
    x_copies = spread(ar_x, x, NX, x_send, x_recv, lambda o: device(z, o, core, y))
    for cp in x_copies:
        cp.wait()
    ar_z[z] = jnp.sum(ar_x[...], axis=0)
    z_copies = spread(ar_z, z, NZ, z_send, z_recv, lambda o: device(o, x, core, y))

    swaps = []
    for c in range(NY):
        drain(gbuf.at[c, :, core], g_recv.at[c])
        cp = remote(gbuf.at[c, :, core], gbuf.at[c, :, core], gx_send.at[c], gx_recv.at[c], partner)
        cp.start()
        swaps.append(cp)
    for cp in swaps:
        cp.wait_recv()

    owner = y // 2
    i_mine = y % 2

    def left_part(n):
        r = 2 * core + n
        acc = jnp.zeros((COLS, WIDTH), F32)
        for c in range(NY):
            rows = gbuf[c, pl.ds(r * 8, 8)].reshape(COLS, COLS)
            acc = acc + lax.dot_general(
                rows, gbuf[c].reshape(WIDTH, COLS), (((1,), (1,)), ((), ())), preferred_element_type=F32
            )
        lb[n] = acc.astype(BF16)

    def right_part(n):
        cols = gbuf[2 * core + n].reshape(WIDTH, COLS)
        for c in range(NY):
            rb[n, :, c * COLS:(c + 1) * COLS] = lax.dot_general(
                cols, gbuf[c].reshape(WIDTH, COLS), (((0,), (0,)), ((), ())), preferred_element_type=F32
            ).astype(BF16)

    def factor_self(n):
        return jnp.logical_and(2 * core + n == y, core == owner)

    def send_factor(m, n, piece):
        rows = pl.ds(pl.multiple_of(piece * ROWS, ROWS), ROWS)
        src = (lb, rb)[m].at[n, rows]
        dst = (left_ref, right_ref)[m].at[i_mine, rows]

        @pl.when(factor_self(n))
        def _():
            pltpu.make_async_copy(src, dst, f_recv.at[m]).start()

        @pl.when(jnp.logical_not(factor_self(n)))
        def _():
            remote(src, dst, f_send.at[m, n], f_recv.at[m], device(z, x, owner, 2 * core + n)).start()

    def send_left(piece, _):
        for n in range(2):
            send_factor(0, n, piece)
        return 0

    for n in range(2):
        left_part(n)
    lax.fori_loop(0, ROWS, send_left, 0)
    for n in range(2):
        right_part(n)

    drain(rrb.at[:, pl.ds(core * half, half)], root_recv.at[1])
    rr_swap = remote(
        rrb.at[:, pl.ds(core * half, half)], rrb.at[:, pl.ds(core * half, half)], rx_send, rx_recv, partner
    )
    rr_swap.start()
    drain(rlb, root_recv.at[0])
    rl = rlb[...].reshape(half, WIDTH)
    for c in range(NY):
        hb[:, c * COLS:(c + 1) * COLS] = jnp.dot(
            rl, gbuf[c].reshape(WIDTH, COLS), preferred_element_type=F32
        ).astype(BF16)
    rr_swap.wait_recv()
    sq = jnp.zeros((8, 128), F32)
    for c in range(NY):
        s = jnp.dot(hb[...], rrb[c], preferred_element_type=F32).astype(BF16)
        sb[c] = s.reshape(NZ * NX, ROWS, COLS)
        s32 = s.astype(F32)
        s2 = jnp.sum((s32 * s32).reshape(half // 8, 8, COLS), axis=0)
        sq = sq + s2[:, :128] + s2[:, 128:]
    for cp in z_copies:
        cp.wait()
    ar_c[core, 0] = sq
    ar_c[core, 1] = jnp.sum(ar_z[...], axis=0)
    c_copy = remote(ar_c.at[core], ar_c.at[core], c_send, c_recv, partner)
    c_copy.start()
    c_copy.wait()
    search_sq = jnp.sum(ar_c[0, 0] + ar_c[1, 0], keepdims=True)
    graft_all = ar_c[0, 1, 0:1] + ar_c[1, 1, 0:1]
    lane = lax.broadcasted_iota(jnp.int32, (1, 128), 1)
    graft_sq = jnp.sum(jnp.where(lane == inv_ref[0, mine], graft_all, 0.0), keepdims=True)
    ratio = jnp.sqrt(graft_sq) / (jnp.sqrt(search_sq) + 1e-06)
    ratio = jnp.broadcast_to(ratio, (1, COLS))

    def scale(k, _):
        few = pl.ds(k * 4, 4)
        for c in range(NY):
            sb[c, few] = (sb[c, few].astype(F32) * ratio).astype(BF16)
        return 0

    lax.fori_loop(0, NZ * NX // 4, scale, 0)

    own_dir = pltpu.make_async_copy(sb.at[y, zx], ubr.at[mine], u_recv)
    own_dir.start()

    def send_dir(k):
        m = k % (NZ * NX) * 13
        tz, tx, ty = (z + m % NZ) % NZ, (x + (m // NZ) % NX) % NX, (y + k // (NZ * NX)) % NY
        remote(
            sb.at[ty, tz * NX + tx], ubr.at[mine], u_send, u_recv, device(tz, tx, core, ty)
        ).start()

    def send_back(n, _):
        for u in range(16):
            @pl.when(n * 16 + u > 0)
            def _(u=u):
                send_dir(n * 16 + u)
        return 0

    def send_right(piece, _):
        for n in range(2):
            send_factor(1, n, piece)
        return 0

    lax.fori_loop(0, 8, send_back, 0)
    lax.fori_loop(0, ROWS, send_right, 0)

    drain(ubr, u_recv)

    drain(left_ref, f_recv.at[0])
    drain(right_ref, f_recv.at[1])
    drain(sbuf.at[pl.ds(0, SLOTS - 1)], g_send)
    drain(ubr.at[pl.ds(0, SLOTS - 1)], u_send)
    for cp in swaps:
        cp.wait_send()
    rr_swap.wait_send()
    for i in range(2):
        for q in range(NC):
            @pl.when(jnp.logical_not(is_self(i, q)))
            def _(i=i, q=q):
                drain(rlb.at[pl.ds(0, 8)], root_send.at[0, i, q])
                drain(rrb.at[0, pl.ds(0, half)], root_send.at[1, i, q])
    for n in range(2):
        @pl.when(jnp.logical_not(factor_self(n)))
        def _(n=n):
            drain(lb.at[n], f_send.at[0, n])
            drain(rb.at[n], f_send.at[1, n])


def exchange(block_slot, gradients, adagrad, root_left, root_right):
    vmem = pl.BlockSpec(memory_space=pltpu.VMEM)
    hbm = pl.BlockSpec(memory_space=pl.ANY)
    dma = pltpu.SemaphoreType.DMA
    return pl.pallas_call(
        kernel,
        out_shape=(
            pltpu.VMEM((SLOTS, ROWS, COLS), BF16),
            pltpu.VMEM((2, COLS, WIDTH), BF16),
            pltpu.VMEM((2, COLS, WIDTH), BF16),
        ),
        in_specs=[vmem, hbm, hbm, hbm, hbm],
        out_specs=(hbm, hbm, hbm),
        scratch_shapes=[
            pltpu.VMEM((NBLK, ROWS, COLS), BF16),
            pltpu.VMEM((NBLK, ROWS, COLS), F32),
            dma((3,)),
            pltpu.SemaphoreType.REGULAR((2,)),
            pltpu.VMEM((8, 128), jnp.int32),
            pltpu.SMEM((8, 128), jnp.int32),
            pltpu.VMEM((SLOTS, ROWS, COLS), BF16),
            pltpu.VMEM((NY, NZ * NX, NC, ROWS, COLS), BF16),
            pltpu.VMEM((NZ * NX, ROWS, WIDTH), BF16),
            pltpu.VMEM((NY, WIDTH, COLS), BF16),
            pltpu.VMEM((WIDTH // 2, WIDTH), BF16),
            pltpu.VMEM((NY, NZ * NX, ROWS, COLS), BF16),
            pltpu.VMEM((2, COLS, WIDTH), BF16),
            pltpu.VMEM((2, COLS, WIDTH), BF16),
            pltpu.VMEM((128, 128), F32),
            pltpu.VMEM((NZ, 8, 128), F32),
            pltpu.VMEM((NX, 8, 128), F32),
            pltpu.VMEM((NY, 8, 128), F32),
            pltpu.VMEM((NC, 2, 8, 128), F32),
            dma, dma((NY,)), dma((NY,)), dma((NY,)), dma((2, 2, NC)), dma((2,)),
            dma, dma, dma((2, 2)), dma((2,)), dma, dma,
            dma((NZ,)), dma((NZ,)), dma((NX,)), dma((NX,)), dma((NY,)), dma((NY,)), dma, dma,
        ],
        compiler_params=pltpu.CompilerParams(
            collective_id=0, has_side_effects=True, vmem_limit_bytes=24 * 2**20
        ),
        cost_estimate=pl.CostEstimate(flops=6 * 10**10, bytes_accessed=6 * 2**20, transcendentals=0),
        name="shampoo_exchange",
    )(block_slot.reshape(1, NBLK), *(in_hbm(v) for v in (gradients, adagrad, root_left, root_right)))


def tail_kernel(
    slot, fl, fr, left, right, g, a, directions, fl_out, fr_out, a_out, upd_out,
    f_buf, t_buf, g_buf, a_buf, f_in, t_in, ga_in, f_sem, a_sem, u_sem,
):
    parts = 4
    rows = 2 * COLS // parts
    ins, outs = [], []
    terms = [pltpu.make_async_copy(src, t_buf.at[m], t_in.at[m]) for m, src in enumerate((left, right))]
    for m, (src, out) in enumerate(((fl, fl_out), (fr, fr_out))):
        for n in range(parts):
            i, r0 = n * rows // COLS, n * rows % COLS
            cut = (i, pl.ds(r0, rows))
            ins.append((m, cut, out, pltpu.make_async_copy(src.at[cut], f_buf.at[(m,) + cut], f_in.at[m, n])))
            ins[-1][-1].start()
        terms[m].start()
    g_copy = pltpu.make_async_copy(g, g_buf, ga_in.at[0])
    a_copy = pltpu.make_async_copy(a, a_buf, ga_in.at[1])
    g_copy.start()
    a_copy.start()

    def place(b, _):
        pltpu.make_async_copy(directions.at[slot[b]], upd_out.at[b], u_sem).start()
        return 0

    lax.fori_loop(0, NBLK, place, 0)
    for n, (m, cut, out, copy) in enumerate(ins):
        copy.wait()
        if n % parts == 0:
            terms[m].wait()
        f_buf[(m,) + cut] = 0.9 * f_buf[(m,) + cut] + 0.1 * t_buf[(m,) + cut].astype(F32)
        outs.append(pltpu.make_async_copy(f_buf.at[(m,) + cut], out.at[cut], f_sem.at[m, n % parts]))
        outs[-1].start()
    g_copy.wait()
    a_copy.wait()

    def add(n, _):
        few = pl.ds(n * 4, 4)
        g32 = g_buf[few].astype(F32)
        a_buf[few] = a_buf[few] + g32 * g32
        return 0

    lax.fori_loop(0, NBLK // 4, add, 0)
    outs.append(pltpu.make_async_copy(a_buf, a_out, a_sem))
    outs[-1].start()
    for copy in outs:
        copy.wait()
    drain(upd_out, u_sem)


def tail(block_slot, factor_left, factor_right, left_term, right_term, gradients, adagrad, directions):
    smem = pl.BlockSpec(memory_space=pltpu.SMEM)
    hbm = pl.BlockSpec(memory_space=pl.ANY)
    dma = pltpu.SemaphoreType.DMA
    return pl.pallas_call(
        tail_kernel,
        out_shape=(
            jax.ShapeDtypeStruct(factor_left.shape, F32),
            jax.ShapeDtypeStruct(factor_right.shape, F32),
            jax.ShapeDtypeStruct(adagrad.shape, F32),
            jax.ShapeDtypeStruct(gradients.shape, BF16),
        ),
        in_specs=[smem] + [hbm] * 7,
        out_specs=(hbm, hbm, hbm, hbm),
        scratch_shapes=[
            pltpu.VMEM((2, 2, COLS, WIDTH), F32),
            pltpu.VMEM((2, 2, COLS, WIDTH), BF16),
            pltpu.VMEM((NBLK, ROWS, COLS), BF16),
            pltpu.VMEM((NBLK, ROWS, COLS), F32),
            dma((2, 4)), dma((2,)), dma((2,)), dma((2, 4)), dma, dma,
        ],
        compiler_params=pltpu.CompilerParams(vmem_limit_bytes=16 * 2**20),
        name="shampoo_tail",
    )(block_slot, factor_left, factor_right, left_term, right_term, gradients, adagrad, directions)


def on_device(gradients, adagrad, factor_left, factor_right, root_left, root_right, block_slot):
    count = factor_left.shape[0]
    directions, left_term, right_term = exchange(
        block_slot, gradients, adagrad, root_left.reshape(count, 8, NC, ROWS, WIDTH), root_right
    )
    factor_left_new, factor_right_new, adagrad_new, update = tail(
        block_slot, factor_left, factor_right, left_term, right_term, gradients, adagrad, directions
    )
    return update, adagrad_new, factor_left_new, factor_right_new


def solution(mesh):
    placed = (
        P(None, "dp", "replica"),
        P(None, "dp", "replica"),
        P("dp", "replica", None),
        P("dp", "replica", None),
        P("dp", "replica", None),
        P("dp", None, "replica"),
        P(),
    )
    return jax.shard_map(
        on_device,
        mesh=mesh,
        in_specs=placed,
        out_specs=(
            P(None, "dp", "replica"),
            P(None, "dp", "replica"),
            P("dp", "replica", None),
            P("dp", "replica", None),
        ),
        check_vma=False,
    )
```

```python
import jax
import jax.numpy as jnp
from jax import lax
from jax.experimental import pallas as pl
from jax.experimental.pallas import tpu as pltpu
from jax.sharding import PartitionSpec as P

MESH = pl.DeviceIdType.MESH
NZ, NX, NC, NY = 8, 4, 2, 4
ROWS, COLS, WIDTH = 16, 256, 1024
SLOTS = NZ * NX * NY
NBLK = 56
F32, BF16 = jnp.float32, jnp.bfloat16


def device(z, x, core, y):
    return (z * (NX * NC) + x * NC + core, y)


def in_hbm(value):
    return pltpu.with_memory_space_constraint(value, pltpu.HBM)


def drain(ref, sem):
    pltpu.make_async_copy(ref, ref, sem).wait()


def kernel(
    slot_hbm, g_hbm, a_hbm, rl_ref, rr_ref,
    ubr, left_ref, right_ref, ratio_ref,
    g_ref, a_ref, in_sem, meet, slot_row, inv_v, inv_ref, sbuf, gbuf, rlb, rrb, hb, sb, lb, rb, gp, ar_z, ar_x, ar_y, ar_c, rt_z, rt_x, rt_y,
    g_send, g_recv, gx_send, gx_recv, root_send, rl_recv, rr_recv,
    rx_send, rx_recv, f_send, f_recv, u_send, u_recv,
    z_send, z_recv, x_send, x_recv, y_send, y_recv, c_send, c_recv,
):
    d = lax.axis_index("dp")
    y = lax.axis_index("replica")
    z, x, core = d // (NX * NC), (d // NC) % NX, d % NC
    other = 1 - core
    zx = z * NX + x
    mine = zx * NY + y
    partner = device(z, x, other, y)

    def target(k):
        m = (k * 37) % SLOTS
        return (z + m % NZ) % NZ, (x + (m // NZ) % NX) % NX, (y + m // (NZ * NX)) % NY

    def remote(src, dst, send, recv, where):
        return pltpu.make_async_remote_copy(
            src_ref=src, dst_ref=dst, send_sem=send, recv_sem=recv,
            device_id=where, device_id_type=MESH,
        )

    loads = [
        pltpu.make_async_copy(g_hbm, g_ref, in_sem.at[0]),
        pltpu.make_async_copy(a_hbm, a_ref, in_sem.at[1]),
        pltpu.make_async_copy(slot_hbm, slot_row, in_sem.at[3]),
    ]
    for cp in loads[::-1]:
        cp.start()

    along_z = [device((z + k) % NZ, x, core, y) for k in range(1, NZ)]
    along_x = [device(z, (x + k) % NX, core, y) for k in range(1, NX)]
    along_y = [device(z, x, core, (y + k) % NY) for k in range(1, NY)]
    barrier = pltpu.get_barrier_semaphore()

    def greet(sem, devices):
        for one in devices:
            pl.semaphore_signal(sem, inc=1, device_id=one, device_id_type=MESH)

    first = along_z + along_x + along_y + [partner]
    greet(barrier, first)

    loads[2].wait()
    at_slot = lax.broadcasted_iota(jnp.int32, (SLOTS, NBLK), 0) == slot_row[...]
    block = lax.broadcasted_iota(jnp.int32, (SLOTS, NBLK), 1)
    block = jnp.min(jnp.where(at_slot, block, NBLK), axis=1, keepdims=True)
    inv_v[...] = jnp.transpose(jnp.broadcast_to(block, (SLOTS, 128)))[:8]
    to_smem = pltpu.make_async_copy(inv_v, inv_ref, in_sem.at[2])
    to_smem.start()

    pl.semaphore_wait(barrier, len(first))
    greet(meet.at[0], along_y)
    to_smem.wait()
    loads[0].wait()
    pl.semaphore_wait(meet.at[0], len(along_y))
    greet(meet.at[1], along_x)

    half = WIDTH // 2

    def pack(t):
        b = inv_ref[0, t]
        rows = g_ref[jnp.clip(b, 0, NBLK - 1)]
        sbuf[t] = jnp.where(b < NBLK, rows, jnp.zeros_like(rows))

    def send_rows(k):
        tz, tx, ty = target(k)
        t = (tz * NX + tx) * NY + ty
        pack(t)
        remote(
            sbuf.at[t], gbuf.at[y, zx, core], g_send, g_recv.at[y], device(tz, tx, core, ty)
        ).start()

    def is_self(i, q):
        return jnp.logical_and(2 * core + i == y, core == q)

    def send_root(i, q, m, n):
        if m == 0:
            src, dst, recv = rl_ref.at[i, n, q], rlb.at[y * 8 + n], rl_recv
        else:
            rows = pl.ds(pl.multiple_of(q * half + n * (half // 8), half // 8), half // 8)
            src, dst, recv = rr_ref.at[i, rows], rrb.at[y, rows], rr_recv.at[y]

        @pl.when(is_self(i, q))
        def _():
            pltpu.make_async_copy(src, dst, recv).start()

        @pl.when(jnp.logical_not(is_self(i, q)))
        def _():
            remote(src, dst, root_send.at[m, i, q], recv, device(z, x, q, 2 * core + i)).start()

    def first_roots(n, _):
        for i, q in [(i, q) for i in range(2) for q in range(NC)]:
            send_root(i, q, 0, n)
        return 0

    lax.fori_loop(0, 2, first_roots, 0)
    pack(mine)
    own_rows = pltpu.make_async_copy(sbuf.at[mine], gbuf.at[y, zx, core], g_recv.at[y])
    own_rows.start()
    pl.semaphore_wait(meet.at[1], len(along_x))

    def send_some(m, first):
        def some(n, _):
            for u in range(16):
                k = (first + n) * 16 + u

                @pl.when(k > 0)
                def _(k=k):
                    send_rows(k)

                if u % 2 == 1:
                    piece = u // 2

                    @pl.when(k >= 16)
                    def _(piece=piece, n=n):
                        send_root(piece // 2 % 2, piece % 2, m, 2 * n + piece // 4)
            return 0

        return some

    lax.fori_loop(0, 4, send_some(0, 0), 0)
    lax.fori_loop(0, 4, send_some(1, 4), 0)

    gp[...] = jnp.zeros_like(gp)

    def graft(b, _):
        g32 = g_ref[b].astype(F32)
        scaled = g32 / (jnp.sqrt(a_ref[b] + g32 * g32) + 1e-08)
        sq = jnp.sum(scaled * scaled, axis=0, keepdims=True)
        gp[pl.ds(b, 1), :] = sq[:, :128] + sq[:, 128:]
        return 0

    loads[1].wait()
    lax.fori_loop(0, NBLK, graft, 0)
    part = jnp.sum(jnp.transpose(gp[...]), axis=0, keepdims=True)
    def spread(buf, me, count, send, recv, where):
        copies = []
        for k in range(1, count):
            other_one = (me + k) % count
            copies.append(remote(buf.at[me], buf.at[me], send.at[k], recv.at[k], where(other_one)))
        for cp in copies:
            cp.start()
        return copies

    def along(axis, buf, value, count, send, recv):
        me = (z, x, y)[axis]
        buf[me] = value
        return spread(buf, me, count, send, recv, lambda o: device(
            o if axis == 0 else z, o if axis == 1 else x, core, o if axis == 2 else y))

    def finish(copies, buf):
        for cp in copies:
            cp.wait()
        return jnp.sum(buf[...], axis=0)

    x_copies = along(1, ar_x, jnp.broadcast_to(part, (8, 128)), NX, x_send.at[0], x_recv.at[0])
    graft_x = finish(x_copies, ar_x)
    z_copies = along(0, ar_z, graft_x, NZ, z_send.at[0], z_recv.at[0])

    swaps = []
    for c in range(NY):
        drain(gbuf.at[c, :, core], g_recv.at[c])
        cp = remote(gbuf.at[c, :, core], gbuf.at[c, :, core], gx_send.at[c], gx_recv.at[c], partner)
        cp.start()
        swaps.append(cp)
    y_copies = along(2, ar_y, finish(z_copies, ar_z), NY, y_send.at[0], y_recv.at[0])
    for cp in swaps:
        cp.wait_recv()

    owner = y // 2
    i_mine = y % 2

    def left_part(n):
        r = 2 * core + n
        acc = jnp.zeros((COLS, WIDTH), F32)
        for c in range(NY):
            rows = gbuf[c, pl.ds(r * 8, 8)].reshape(COLS, COLS)
            acc = acc + lax.dot_general(
                rows, gbuf[c].reshape(WIDTH, COLS), (((1,), (1,)), ((), ())), preferred_element_type=F32
            )
        lb[n] = acc.astype(BF16)

    def right_part(n):
        cols = gbuf[2 * core + n].reshape(WIDTH, COLS)
        for c in range(NY):
            rb[n, :, c * COLS:(c + 1) * COLS] = lax.dot_general(
                cols, gbuf[c].reshape(WIDTH, COLS), (((0,), (0,)), ((), ())), preferred_element_type=F32
            ).astype(BF16)

    def factor_self(n):
        return jnp.logical_and(2 * core + n == y, core == owner)

    def send_factor(m, n, piece):
        rows = pl.ds(pl.multiple_of(piece * ROWS, ROWS), ROWS)
        src = (lb, rb)[m].at[n, rows]
        dst = (left_ref, right_ref)[m].at[i_mine, rows]

        @pl.when(factor_self(n))
        def _():
            pltpu.make_async_copy(src, dst, f_recv.at[m]).start()

        @pl.when(jnp.logical_not(factor_self(n)))
        def _():
            remote(src, dst, f_send.at[m, n], f_recv.at[m], device(z, x, owner, 2 * core + n)).start()

    def send_left(piece, _):
        for n in range(2):
            send_factor(0, n, piece)
        return 0

    for n in range(2):
        left_part(n)
    lax.fori_loop(0, ROWS, send_left, 0)
    for n in range(2):
        right_part(n)

    drain(rlb, rl_recv)
    rl = rlb[...].reshape(half, WIDTH)
    for c in range(NY):
        hb[:, c * COLS:(c + 1) * COLS] = jnp.dot(
            rl, gbuf[c].reshape(WIDTH, COLS), preferred_element_type=F32
        ).astype(BF16)

    def swap_root(c):
        part = rrb.at[c, pl.ds(pl.multiple_of(core * half, half), half)]
        drain(part, rr_recv.at[c])
        cp = remote(part, part, rx_send.at[c], rx_recv.at[c], partner)
        cp.start()
        return cp

    def send_back(c):
        def one(k, _):
            m = k * 13
            tz, tx = (z + m % NZ) % NZ, (x + (m // NZ) % NX) % NX
            remote(
                sb.at[c, tz * NX + tx], ubr.at[mine], u_send, u_recv, device(tz, tx, core, c)
            ).start()
            return 0

        return one

    sq = jnp.zeros((8, 128), F32)
    quarters = [(y + k) % NY for k in (0, 1, 3, 2)]
    root_swaps = [swap_root(quarters[0])]
    for k, c in enumerate(quarters):
        if k + 1 < NY:
            root_swaps.append(swap_root(quarters[k + 1]))
        root_swaps[k].wait_recv()
        s = jnp.dot(hb[...], rrb[c], preferred_element_type=F32).astype(BF16)
        sb[c] = s.reshape(NZ * NX, ROWS, COLS)
        if k == 0:
            own_dir = pltpu.make_async_copy(sb.at[y, zx], ubr.at[mine], u_recv)
            own_dir.start()
        lax.fori_loop(1 if k == 0 else 0, NZ * NX, send_back(c), 0)
        s32 = s.astype(F32)
        s2 = jnp.sum((s32 * s32).reshape(half // 8, 8, COLS), axis=0)
        sq = sq + s2[:, :128] + s2[:, 128:]

    ar_c[core, 0] = sq
    ar_c[core, 1] = finish(y_copies, ar_y)
    c_copy = remote(ar_c.at[core], ar_c.at[core], c_send, c_recv, partner)
    c_copy.start()
    c_copy.wait()
    search_sq = jnp.sum(ar_c[0, 0] + ar_c[1, 0], keepdims=True)
    graft_all = ar_c[0, 1] + ar_c[1, 1]
    lane = lax.broadcasted_iota(jnp.int32, (8, 128), 1)
    graft_sq = jnp.sum(jnp.where(lane[:1] == inv_ref[0, mine], graft_all[:1], 0.0), keepdims=True)
    ratio = jnp.sqrt(graft_sq) / (jnp.sqrt(search_sq) + 1e-06)
    ratio = jnp.where(lane == mine, jnp.broadcast_to(ratio, (8, 128)), 0.0)
    x_ratio = finish(along(1, rt_x, ratio, NX, x_send.at[1], x_recv.at[1]), rt_x)
    y_ratio = along(2, rt_y, x_ratio, NY, y_send.at[1], y_recv.at[1])

    def send_right(piece, _):
        for n in range(2):
            send_factor(1, n, piece)
        return 0

    lax.fori_loop(0, ROWS, send_right, 0)
    z_ratio = along(0, rt_z, finish(y_ratio, rt_y), NZ, z_send.at[1], z_recv.at[1])
    ratio_ref[...] = finish(z_ratio, rt_z)
    drain(ubr, u_recv)

    drain(left_ref, f_recv.at[0])
    drain(right_ref, f_recv.at[1])
    drain(sbuf.at[pl.ds(0, SLOTS - 1)], g_send)
    drain(ubr.at[pl.ds(0, SLOTS - 1)], u_send)
    for cp in swaps:
        cp.wait_send()
    for cp in root_swaps:
        cp.wait_send()
    for i in range(2):
        for q in range(NC):
            @pl.when(jnp.logical_not(is_self(i, q)))
            def _(i=i, q=q):
                drain(rlb.at[pl.ds(0, 8)], root_send.at[0, i, q])
                drain(rrb.at[0, pl.ds(0, half)], root_send.at[1, i, q])
    for n in range(2):
        @pl.when(jnp.logical_not(factor_self(n)))
        def _(n=n):
            drain(lb.at[n], f_send.at[0, n])
            drain(rb.at[n], f_send.at[1, n])


def exchange(block_slot, gradients, adagrad, root_left, root_right):
    vmem = pl.BlockSpec(memory_space=pltpu.VMEM)
    hbm = pl.BlockSpec(memory_space=pl.ANY)
    dma = pltpu.SemaphoreType.DMA
    return pl.pallas_call(
        kernel,
        out_shape=(
            pltpu.VMEM((SLOTS, ROWS, COLS), BF16),
            pltpu.VMEM((2, COLS, WIDTH), BF16),
            pltpu.VMEM((2, COLS, WIDTH), BF16),
            jax.ShapeDtypeStruct((8, 128), F32),
        ),
        in_specs=[hbm] * 5,
        out_specs=(hbm, hbm, hbm, vmem),
        scratch_shapes=[
            pltpu.VMEM((NBLK, ROWS, COLS), BF16),
            pltpu.VMEM((NBLK, ROWS, COLS), F32),
            dma((4,)),
            pltpu.SemaphoreType.REGULAR((2,)),
            pltpu.VMEM((1, NBLK), jnp.int32),
            pltpu.VMEM((8, 128), jnp.int32),
            pltpu.SMEM((8, 128), jnp.int32),
            pltpu.VMEM((SLOTS, ROWS, COLS), BF16),
            pltpu.VMEM((NY, NZ * NX, NC, ROWS, COLS), BF16),
            pltpu.VMEM((NZ * NX, ROWS, WIDTH), BF16),
            pltpu.VMEM((NY, WIDTH, COLS), BF16),
            pltpu.VMEM((WIDTH // 2, WIDTH), BF16),
            pltpu.VMEM((NY, NZ * NX, ROWS, COLS), BF16),
            pltpu.VMEM((2, COLS, WIDTH), BF16),
            pltpu.VMEM((2, COLS, WIDTH), BF16),
            pltpu.VMEM((128, 128), F32),
            pltpu.VMEM((NZ, 8, 128), F32),
            pltpu.VMEM((NX, 8, 128), F32),
            pltpu.VMEM((NY, 8, 128), F32),
            pltpu.VMEM((NC, 2, 8, 128), F32),
            pltpu.VMEM((NZ, 8, 128), F32),
            pltpu.VMEM((NX, 8, 128), F32),
            pltpu.VMEM((NY, 8, 128), F32),
            dma, dma((NY,)), dma((NY,)), dma((NY,)), dma((2, 2, NC)), dma, dma((NY,)),
            dma((NY,)), dma((NY,)), dma((2, 2)), dma((2,)), dma, dma,
            dma((2, NZ)), dma((2, NZ)), dma((2, NX)), dma((2, NX)), dma((2, NY)), dma((2, NY)), dma, dma,
        ],
        compiler_params=pltpu.CompilerParams(
            collective_id=0, has_side_effects=True, vmem_limit_bytes=24 * 2**20
        ),
        cost_estimate=pl.CostEstimate(flops=6 * 10**10, bytes_accessed=6 * 2**20, transcendentals=0),
        name="shampoo_exchange",
    )(*(in_hbm(v) for v in (block_slot.reshape(1, NBLK), gradients, adagrad, root_left, root_right)))


def tail_kernel(
    slot, ratio_v, fl, fr, left, right, g, a, directions, fl_out, fr_out, a_out, upd_out,
    f_buf, a_buf, u_buf, ratio, f_sem, a_sem, u_sem, r_sem,
):
    outs = []

    to_smem = pltpu.make_async_copy(ratio_v, ratio, r_sem)
    to_smem.start()
    parts = 4
    rows = 2 * COLS // parts
    for m, (old, term, out) in enumerate(((fl, left, fl_out), (fr, right, fr_out))):
        for n in range(parts):
            cut = (n * rows // COLS, pl.ds(n * rows % COLS, rows))
            f_buf[(m,) + cut] = 0.9 * old[cut] + 0.1 * term[cut].astype(F32)
            outs.append(pltpu.make_async_copy(f_buf.at[(m,) + cut], out.at[cut], f_sem.at[m, n]))
            outs[-1].start()

    to_smem.wait()

    def scale(b, _):
        t = slot[b]
        u_buf[b] = (directions[t].astype(F32) * ratio[0, t]).astype(BF16)
        return 0

    lax.fori_loop(0, NBLK, scale, 0)
    outs.append(pltpu.make_async_copy(u_buf, upd_out, u_sem))
    outs[-1].start()

    def add(n, _):
        few = pl.ds(n * 4, 4)
        g32 = g[few].astype(F32)
        a_buf[few] = a[few] + g32 * g32
        return 0

    lax.fori_loop(0, NBLK // 4, add, 0)
    outs.append(pltpu.make_async_copy(a_buf, a_out, a_sem))
    outs[-1].start()
    for copy in outs:
        copy.wait()


def tail(block_slot, ratio, factor_left, factor_right, left_term, right_term, gradients, adagrad, directions):
    smem = pl.BlockSpec(memory_space=pltpu.SMEM)
    vmem = pl.BlockSpec(memory_space=pltpu.VMEM)
    hbm = pl.BlockSpec(memory_space=pl.ANY)
    dma = pltpu.SemaphoreType.DMA
    return pl.pallas_call(
        tail_kernel,
        out_shape=(
            jax.ShapeDtypeStruct(factor_left.shape, F32),
            jax.ShapeDtypeStruct(factor_right.shape, F32),
            jax.ShapeDtypeStruct(adagrad.shape, F32),
            jax.ShapeDtypeStruct(gradients.shape, BF16),
        ),
        in_specs=[smem] + [vmem] * 8,
        out_specs=(hbm, hbm, hbm, hbm),
        scratch_shapes=[
            pltpu.VMEM((2, 2, COLS, WIDTH), F32),
            pltpu.VMEM((NBLK, ROWS, COLS), F32),
            pltpu.VMEM((NBLK, ROWS, COLS), BF16),
            pltpu.SMEM((8, 128), F32),
            dma((2, 4)), dma, dma, dma,
        ],
        compiler_params=pltpu.CompilerParams(vmem_limit_bytes=24 * 2**20),
        name="shampoo_tail",
    )(block_slot, ratio, factor_left, factor_right, left_term, right_term, gradients, adagrad, directions)


def on_device(gradients, adagrad, factor_left, factor_right, root_left, root_right, block_slot):
    count = factor_left.shape[0]
    directions, left_term, right_term, ratio = exchange(
        block_slot, gradients, adagrad, root_left.reshape(count, 8, NC, ROWS, WIDTH), root_right
    )
    factor_left_new, factor_right_new, adagrad_new, update = tail(
        block_slot, ratio, factor_left, factor_right, left_term, right_term, gradients, adagrad, directions
    )
    return update, adagrad_new, factor_left_new, factor_right_new


def solution(mesh):
    placed = (
        P(None, "dp", "replica"),
        P(None, "dp", "replica"),
        P("dp", "replica", None),
        P("dp", "replica", None),
        P("dp", "replica", None),
        P("dp", None, "replica"),
        P(),
    )
    return jax.shard_map(
        on_device,
        mesh=mesh,
        in_specs=placed,
        out_specs=(
            P(None, "dp", "replica"),
            P(None, "dp", "replica"),
            P("dp", "replica", None),
            P("dp", "replica", None),
        ),
        check_vma=False,
    )
```

```python
import jax
import jax.numpy as jnp
from jax import lax
from jax.experimental import pallas as pl
from jax.experimental.pallas import tpu as pltpu
from jax.sharding import PartitionSpec as P

MESH = pl.DeviceIdType.MESH
NZ, NX, NC, NY = 8, 4, 2, 4
ROWS, COLS, WIDTH = 16, 256, 1024
SLOTS = NZ * NX * NY
NBLK = 56
F32, BF16 = jnp.float32, jnp.bfloat16


def device(z, x, core, y):
    return (z * (NX * NC) + x * NC + core, y)


def in_hbm(value):
    return pltpu.with_memory_space_constraint(value, pltpu.HBM)


def drain(ref, sem):
    pltpu.make_async_copy(ref, ref, sem).wait()


def kernel(
    slot_hbm, g_hbm, a_hbm, rl_ref, rr_ref,
    ubr, left_ref, right_ref, ratio_ref,
    g_ref, a_ref, in_sem, meet, slot_row, inv_v, inv_ref, sbuf, gbuf, rlb, rrb, hb, sb, lb, rb, gp, ar_z, ar_x, ar_y, ar_c, rt_z, rt_x, rt_y,
    g_send, g_recv, gx_send, gx_recv, root_send, rl_recv, rr_recv,
    rx_send, rx_recv, f_send, f_recv, u_send, u_recv,
    z_send, z_recv, x_send, x_recv, y_send, y_recv, c_send, c_recv,
):
    d = lax.axis_index("dp")
    y = lax.axis_index("replica")
    z, x, core = d // (NX * NC), (d // NC) % NX, d % NC
    other = 1 - core
    zx = z * NX + x
    mine = zx * NY + y
    partner = device(z, x, other, y)

    def target(k):
        m = (k * 37) % SLOTS
        return (z + m % NZ) % NZ, (x + (m // NZ) % NX) % NX, (y + m // (NZ * NX)) % NY

    def remote(src, dst, send, recv, where):
        return pltpu.make_async_remote_copy(
            src_ref=src, dst_ref=dst, send_sem=send, recv_sem=recv,
            device_id=where, device_id_type=MESH,
        )

    loads = [
        pltpu.make_async_copy(g_hbm, g_ref, in_sem.at[0]),
        pltpu.make_async_copy(a_hbm, a_ref, in_sem.at[1]),
        pltpu.make_async_copy(slot_hbm, slot_row, in_sem.at[3]),
    ]
    for cp in loads[::-1]:
        cp.start()

    along_z = [device((z + k) % NZ, x, core, y) for k in range(1, NZ)]
    along_x = [device(z, (x + k) % NX, core, y) for k in range(1, NX)]
    along_y = [device(z, x, core, (y + k) % NY) for k in range(1, NY)]
    barrier = pltpu.get_barrier_semaphore()

    def greet(sem, devices):
        for one in devices:
            pl.semaphore_signal(sem, inc=1, device_id=one, device_id_type=MESH)

    first = along_z + along_x + along_y + [partner]
    greet(barrier, first)

    loads[2].wait()
    at_slot = lax.broadcasted_iota(jnp.int32, (SLOTS, NBLK), 0) == slot_row[...]
    block = lax.broadcasted_iota(jnp.int32, (SLOTS, NBLK), 1)
    block = jnp.min(jnp.where(at_slot, block, NBLK), axis=1, keepdims=True)
    inv_v[...] = jnp.transpose(jnp.broadcast_to(block, (SLOTS, 128)))[:8]
    to_smem = pltpu.make_async_copy(inv_v, inv_ref, in_sem.at[2])
    to_smem.start()

    pl.semaphore_wait(barrier, len(first))
    greet(meet.at[0], along_y)
    to_smem.wait()
    loads[0].wait()
    pl.semaphore_wait(meet.at[0], len(along_y))
    greet(meet.at[1], along_x)

    half = WIDTH // 2

    def pack(t):
        b = inv_ref[0, t]
        rows = g_ref[jnp.clip(b, 0, NBLK - 1)]
        sbuf[t] = jnp.where(b < NBLK, rows, jnp.zeros_like(rows))

    def send_rows(k):
        tz, tx, ty = target(k)
        t = (tz * NX + tx) * NY + ty
        pack(t)
        remote(
            sbuf.at[t], gbuf.at[y, zx, core], g_send, g_recv.at[y], device(tz, tx, core, ty)
        ).start()

    def is_self(i, q):
        return jnp.logical_and(2 * core + i == y, core == q)

    def send_root(i, q, m, n):
        if m == 0:
            src, dst, recv = rl_ref.at[i, n, q], rlb.at[y * 8 + n], rl_recv
        else:
            rows = pl.ds(pl.multiple_of(q * half + n * (half // 8), half // 8), half // 8)
            src, dst, recv = rr_ref.at[i, rows], rrb.at[y, rows], rr_recv.at[y]

        @pl.when(is_self(i, q))
        def _():
            pltpu.make_async_copy(src, dst, recv).start()

        @pl.when(jnp.logical_not(is_self(i, q)))
        def _():
            remote(src, dst, root_send.at[m, i, q], recv, device(z, x, q, 2 * core + i)).start()

    def first_roots(n, _):
        for i, q in [(i, q) for i in range(2) for q in range(NC)]:
            send_root(i, q, 0, n)
        return 0

    lax.fori_loop(0, 2, first_roots, 0)
    pack(mine)
    own_rows = pltpu.make_async_copy(sbuf.at[mine], gbuf.at[y, zx, core], g_recv.at[y])
    own_rows.start()
    pl.semaphore_wait(meet.at[1], len(along_x))

    def send_some(m, first):
        def some(n, _):
            for u in range(16):
                k = (first + n) * 16 + u

                @pl.when(k > 0)
                def _(k=k):
                    send_rows(k)

                if u % 2 == 1:
                    piece = u // 2

                    @pl.when(k >= 16)
                    def _(piece=piece, n=n):
                        send_root(piece // 2 % 2, piece % 2, m, 2 * n + piece // 4)
            return 0

        return some

    lax.fori_loop(0, 4, send_some(0, 0), 0)
    lax.fori_loop(0, 4, send_some(1, 4), 0)

    gp[...] = jnp.zeros_like(gp)

    def graft(b, _):
        g32 = g_ref[b].astype(F32)
        scaled = g32 / (jnp.sqrt(a_ref[b] + g32 * g32) + 1e-08)
        sq = jnp.sum(scaled * scaled, axis=0, keepdims=True)
        gp[pl.ds(b, 1), :] = sq[:, :128] + sq[:, 128:]
        return 0

    loads[1].wait()
    lax.fori_loop(0, NBLK, graft, 0)
    part = jnp.sum(jnp.transpose(gp[...]), axis=0, keepdims=True)
    def spread(buf, me, count, send, recv, where):
        copies = []
        for k in range(1, count):
            other_one = (me + k) % count
            copies.append(remote(buf.at[me], buf.at[me], send.at[k], recv.at[k], where(other_one)))
        for cp in copies:
            cp.start()
        return copies

    def along(axis, buf, value, count, send, recv):
        me = (z, x, y)[axis]
        buf[me] = value
        return spread(buf, me, count, send, recv, lambda o: device(
            o if axis == 0 else z, o if axis == 1 else x, core, o if axis == 2 else y))

    def finish(copies, buf):
        for cp in copies:
            cp.wait()
        return jnp.sum(buf[...], axis=0)

    x_copies = along(1, ar_x, jnp.broadcast_to(part, (8, 128)), NX, x_send.at[0], x_recv.at[0])
    graft_x = finish(x_copies, ar_x)
    z_copies = along(0, ar_z, graft_x, NZ, z_send.at[0], z_recv.at[0])

    swaps = []
    for c in range(NY):
        drain(gbuf.at[c, :, core], g_recv.at[c])
        cp = remote(gbuf.at[c, :, core], gbuf.at[c, :, core], gx_send.at[c], gx_recv.at[c], partner)
        cp.start()
        swaps.append(cp)
    y_copies = along(2, ar_y, finish(z_copies, ar_z), NY, y_send.at[0], y_recv.at[0])
    for cp in swaps:
        cp.wait_recv()

    owner = y // 2
    i_mine = y % 2

    def left_part(n):
        r = 2 * core + n
        for k in range(NY):
            acc = jnp.zeros((COLS, COLS), F32)
            for c in range(NY):
                acc = acc + lax.dot_general(
                    gbuf[c, pl.ds(r * 8, 8)].reshape(COLS, COLS),
                    gbuf[c, pl.ds((r + k) % NY * 8, 8)].reshape(COLS, COLS),
                    (((1,), (1,)), ((), ())), preferred_element_type=F32,
                )
            lb[n, :, k * COLS:(k + 1) * COLS] = acc.astype(BF16)

    def right_part(n):
        r = 2 * core + n
        for k in range(NY):
            rb[n, :, k * COLS:(k + 1) * COLS] = lax.dot_general(
                gbuf[r].reshape(WIDTH, COLS), gbuf[(r + k) % NY].reshape(WIDTH, COLS),
                (((0,), (0,)), ((), ())), preferred_element_type=F32,
            ).astype(BF16)

    def factor_self(n):
        return jnp.logical_and(2 * core + n == y, core == owner)

    def send_factor(m, n, piece, skip):
        rows = pl.ds(pl.multiple_of(piece * ROWS, ROWS), ROWS)
        columns = pl.ds(skip, WIDTH - skip)
        src = (lb, rb)[m].at[n, rows, columns]
        dst = (left_ref, right_ref)[m].at[i_mine, rows, columns]

        @pl.when(factor_self(n))
        def _():
            pltpu.make_async_copy(src, dst, f_recv.at[m]).start()

        @pl.when(jnp.logical_not(factor_self(n)))
        def _():
            remote(src, dst, f_send.at[m, n], f_recv.at[m], device(z, x, owner, 2 * core + n)).start()

    def send_terms(m):
        def upper(piece, _):
            for n in range(2):
                send_factor(m, n, piece, 0)
            return 0

        def lower(piece, _):
            for n in range(2):
                send_factor(m, n, piece, COLS // 2)
            return 0

        lax.fori_loop(0, ROWS // 2, upper, 0)
        lax.fori_loop(ROWS // 2, ROWS, lower, 0)

    for n in range(2):
        left_part(n)
    send_terms(0)
    for n in range(2):
        right_part(n)

    drain(rlb, rl_recv)
    rl = rlb[...].reshape(half, WIDTH)
    for c in range(NY):
        hb[:, c * COLS:(c + 1) * COLS] = jnp.dot(
            rl, gbuf[c].reshape(WIDTH, COLS), preferred_element_type=F32
        ).astype(BF16)

    def swap_root(c):
        part = rrb.at[c, pl.ds(pl.multiple_of(core * half, half), half)]
        drain(part, rr_recv.at[c])
        cp = remote(part, part, rx_send.at[c], rx_recv.at[c], partner)
        cp.start()
        return cp

    def send_back(c):
        def one(k, _):
            m = k * 13
            tz, tx = (z + m % NZ) % NZ, (x + (m // NZ) % NX) % NX
            remote(
                sb.at[c, tz * NX + tx], ubr.at[mine], u_send, u_recv, device(tz, tx, core, c)
            ).start()
            return 0

        return one

    sq = jnp.zeros((8, 128), F32)
    quarters = [(y + k) % NY for k in (0, 1, 3, 2)]
    root_swaps = [swap_root(quarters[0])]
    for k, c in enumerate(quarters):
        if k + 1 < NY:
            root_swaps.append(swap_root(quarters[k + 1]))
        root_swaps[k].wait_recv()
        s = jnp.dot(hb[...], rrb[c], preferred_element_type=F32).astype(BF16)
        sb[c] = s.reshape(NZ * NX, ROWS, COLS)
        if k == 0:
            own_dir = pltpu.make_async_copy(sb.at[y, zx], ubr.at[mine], u_recv)
            own_dir.start()
        lax.fori_loop(1 if k == 0 else 0, NZ * NX, send_back(c), 0)
        s32 = s.astype(F32)
        s2 = jnp.sum((s32 * s32).reshape(half // 8, 8, COLS), axis=0)
        sq = sq + s2[:, :128] + s2[:, 128:]

    ar_c[core, 0] = sq
    ar_c[core, 1] = finish(y_copies, ar_y)
    c_copy = remote(ar_c.at[core], ar_c.at[core], c_send, c_recv, partner)
    c_copy.start()
    c_copy.wait()
    search_sq = jnp.sum(ar_c[0, 0] + ar_c[1, 0], keepdims=True)
    graft_all = ar_c[0, 1] + ar_c[1, 1]
    lane = lax.broadcasted_iota(jnp.int32, (8, 128), 1)
    graft_sq = jnp.sum(jnp.where(lane[:1] == inv_ref[0, mine], graft_all[:1], 0.0), keepdims=True)
    ratio = jnp.sqrt(graft_sq) / (jnp.sqrt(search_sq) + 1e-06)
    ratio = jnp.where(lane == mine, jnp.broadcast_to(ratio, (8, 128)), 0.0)
    x_ratio = finish(along(1, rt_x, ratio, NX, x_send.at[1], x_recv.at[1]), rt_x)
    y_ratio = along(2, rt_y, x_ratio, NY, y_send.at[1], y_recv.at[1])

    send_terms(1)
    z_ratio = along(0, rt_z, finish(y_ratio, rt_y), NZ, z_send.at[1], z_recv.at[1])
    ratio_ref[...] = finish(z_ratio, rt_z)
    drain(ubr, u_recv)

    drain(sbuf.at[pl.ds(0, 120)], f_recv.at[0])
    drain(sbuf.at[pl.ds(0, 120)], f_recv.at[1])
    drain(sbuf.at[pl.ds(0, SLOTS - 1)], g_send)
    drain(ubr.at[pl.ds(0, SLOTS - 1)], u_send)
    for cp in swaps:
        cp.wait_send()
    for cp in root_swaps:
        cp.wait_send()
    for i in range(2):
        for q in range(NC):
            @pl.when(jnp.logical_not(is_self(i, q)))
            def _(i=i, q=q):
                drain(rlb.at[pl.ds(0, 8)], root_send.at[0, i, q])
                drain(rrb.at[0, pl.ds(0, half)], root_send.at[1, i, q])
    for n in range(2):
        @pl.when(jnp.logical_not(factor_self(n)))
        def _(n=n):
            drain(sbuf.at[pl.ds(0, 60)], f_send.at[0, n])
            drain(sbuf.at[pl.ds(0, 60)], f_send.at[1, n])


def exchange(block_slot, gradients, adagrad, root_left, root_right):
    vmem = pl.BlockSpec(memory_space=pltpu.VMEM)
    hbm = pl.BlockSpec(memory_space=pl.ANY)
    dma = pltpu.SemaphoreType.DMA
    return pl.pallas_call(
        kernel,
        out_shape=(
            pltpu.VMEM((SLOTS, ROWS, COLS), BF16),
            pltpu.VMEM((2, COLS, WIDTH), BF16),
            pltpu.VMEM((2, COLS, WIDTH), BF16),
            jax.ShapeDtypeStruct((8, 128), F32),
        ),
        in_specs=[hbm] * 5,
        out_specs=(hbm, hbm, hbm, vmem),
        scratch_shapes=[
            pltpu.VMEM((NBLK, ROWS, COLS), BF16),
            pltpu.VMEM((NBLK, ROWS, COLS), F32),
            dma((4,)),
            pltpu.SemaphoreType.REGULAR((2,)),
            pltpu.VMEM((1, NBLK), jnp.int32),
            pltpu.VMEM((8, 128), jnp.int32),
            pltpu.SMEM((8, 128), jnp.int32),
            pltpu.VMEM((SLOTS, ROWS, COLS), BF16),
            pltpu.VMEM((NY, NZ * NX, NC, ROWS, COLS), BF16),
            pltpu.VMEM((NZ * NX, ROWS, WIDTH), BF16),
            pltpu.VMEM((NY, WIDTH, COLS), BF16),
            pltpu.VMEM((WIDTH // 2, WIDTH), BF16),
            pltpu.VMEM((NY, NZ * NX, ROWS, COLS), BF16),
            pltpu.VMEM((2, COLS, WIDTH), BF16),
            pltpu.VMEM((2, COLS, WIDTH), BF16),
            pltpu.VMEM((128, 128), F32),
            pltpu.VMEM((NZ, 8, 128), F32),
            pltpu.VMEM((NX, 8, 128), F32),
            pltpu.VMEM((NY, 8, 128), F32),
            pltpu.VMEM((NC, 2, 8, 128), F32),
            pltpu.VMEM((NZ, 8, 128), F32),
            pltpu.VMEM((NX, 8, 128), F32),
            pltpu.VMEM((NY, 8, 128), F32),
            dma, dma((NY,)), dma((NY,)), dma((NY,)), dma((2, 2, NC)), dma, dma((NY,)),
            dma((NY,)), dma((NY,)), dma((2, 2)), dma((2,)), dma, dma,
            dma((2, NZ)), dma((2, NZ)), dma((2, NX)), dma((2, NX)), dma((2, NY)), dma((2, NY)), dma, dma,
        ],
        compiler_params=pltpu.CompilerParams(
            collective_id=0, has_side_effects=True, vmem_limit_bytes=24 * 2**20
        ),
        cost_estimate=pl.CostEstimate(flops=6 * 10**10, bytes_accessed=6 * 2**20, transcendentals=0),
        name="shampoo_exchange",
    )(*(in_hbm(v) for v in (block_slot.reshape(1, NBLK), gradients, adagrad, root_left, root_right)))


def tail_kernel(
    slot, ratio_v, fl, fr, left, right, g, a, directions, fl_out, fr_out, a_out, upd_out,
    f_buf, a_buf, u_buf, ratio, f_sem, a_sem, u_sem, r_sem,
):
    outs = []

    to_smem = pltpu.make_async_copy(ratio_v, ratio, r_sem)
    to_smem.start()
    y = lax.axis_index("replica")
    half = COLS // 2
    for m, (old, term, out) in enumerate(((fl, left, fl_out), (fr, right, fr_out))):
        for n in range(4):
            i, low = n // 2, n % 2
            rows = pl.ds(low * half, half)
            for k in range(NY):
                columns = pl.ds(pl.multiple_of((y + k) % NY * COLS, COLS), COLS)
                if k == 0 and low:
                    mirrored = jnp.transpose(term[i, :half, half:COLS].astype(F32))
                    new = jnp.concatenate([mirrored, term[i, half:, half:COLS].astype(F32)], axis=1)
                else:
                    new = term[i, rows, k * COLS:(k + 1) * COLS].astype(F32)
                f_buf[m, i, rows, columns] = 0.9 * old[i, rows, columns] + 0.1 * new
            outs.append(pltpu.make_async_copy(f_buf.at[m, i, rows], out.at[i, rows], f_sem.at[m, n]))
            outs[-1].start()

    to_smem.wait()

    def scale(b, _):
        t = slot[b]
        u_buf[b] = (directions[t].astype(F32) * ratio[0, t]).astype(BF16)
        return 0

    lax.fori_loop(0, NBLK, scale, 0)
    outs.append(pltpu.make_async_copy(u_buf, upd_out, u_sem))
    outs[-1].start()

    def add(n, _):
        few = pl.ds(n * 4, 4)
        g32 = g[few].astype(F32)
        a_buf[few] = a[few] + g32 * g32
        return 0

    lax.fori_loop(0, NBLK // 4, add, 0)
    outs.append(pltpu.make_async_copy(a_buf, a_out, a_sem))
    outs[-1].start()
    for copy in outs:
        copy.wait()


def tail(block_slot, ratio, factor_left, factor_right, left_term, right_term, gradients, adagrad, directions):
    smem = pl.BlockSpec(memory_space=pltpu.SMEM)
    vmem = pl.BlockSpec(memory_space=pltpu.VMEM)
    hbm = pl.BlockSpec(memory_space=pl.ANY)
    dma = pltpu.SemaphoreType.DMA
    return pl.pallas_call(
        tail_kernel,
        out_shape=(
            jax.ShapeDtypeStruct(factor_left.shape, F32),
            jax.ShapeDtypeStruct(factor_right.shape, F32),
            jax.ShapeDtypeStruct(adagrad.shape, F32),
            jax.ShapeDtypeStruct(gradients.shape, BF16),
        ),
        in_specs=[smem] + [vmem] * 8,
        out_specs=(hbm, hbm, hbm, hbm),
        scratch_shapes=[
            pltpu.VMEM((2, 2, COLS, WIDTH), F32),
            pltpu.VMEM((NBLK, ROWS, COLS), F32),
            pltpu.VMEM((NBLK, ROWS, COLS), BF16),
            pltpu.SMEM((8, 128), F32),
            dma((2, 4)), dma, dma, dma,
        ],
        compiler_params=pltpu.CompilerParams(vmem_limit_bytes=24 * 2**20),
        name="shampoo_tail",
    )(block_slot, ratio, factor_left, factor_right, left_term, right_term, gradients, adagrad, directions)


def on_device(gradients, adagrad, factor_left, factor_right, root_left, root_right, block_slot):
    count = factor_left.shape[0]
    directions, left_term, right_term, ratio = exchange(
        block_slot, gradients, adagrad, root_left.reshape(count, 8, NC, ROWS, WIDTH), root_right
    )
    factor_left_new, factor_right_new, adagrad_new, update = tail(
        block_slot, ratio, factor_left, factor_right, left_term, right_term, gradients, adagrad, directions
    )
    return update, adagrad_new, factor_left_new, factor_right_new


def solution(mesh):
    placed = (
        P(None, "dp", "replica"),
        P(None, "dp", "replica"),
        P("dp", "replica", None),
        P("dp", "replica", None),
        P("dp", "replica", None),
        P("dp", None, "replica"),
        P(),
    )
    return jax.shard_map(
        on_device,
        mesh=mesh,
        in_specs=placed,
        out_specs=(
            P(None, "dp", "replica"),
            P(None, "dp", "replica"),
            P("dp", "replica", None),
            P("dp", "replica", None),
        ),
        check_vma=False,
    )
```

```python
import jax
import jax.numpy as jnp
from jax import lax
from jax.experimental import pallas as pl
from jax.experimental.pallas import tpu as pltpu
from jax.sharding import PartitionSpec as P

MESH = pl.DeviceIdType.MESH
NZ, NX, NC, NY = 8, 4, 2, 4
ROWS, COLS, WIDTH = 16, 256, 1024
SLOTS = NZ * NX * NY
NBLK = 56
F32, BF16 = jnp.float32, jnp.bfloat16


def device(z, x, core, y):
    return (z * (NX * NC) + x * NC + core, y)


def in_hbm(value):
    return pltpu.with_memory_space_constraint(value, pltpu.HBM)


def drain(ref, sem):
    pltpu.make_async_copy(ref, ref, sem).wait()


def kernel(
    slot_hbm, g_hbm, a_hbm, rl_ref, rr_ref,
    ubr, left_ref, right_ref, ratio_ref,
    g_ref, a_ref, in_sem, meet, slot_row, inv_v, inv_ref, sbuf, gbuf, rlb, rrb, hb, sb, lb, rb, gp, ar_z, ar_x, ar_y, ar_c, rt_z, rt_x, rt_y,
    g_send, g_recv, gx_send, gx_recv, root_send, rl_recv, rr_recv,
    rx_send, rx_recv, f_send, f_recv, u_send, u_recv,
    z_send, z_recv, x_send, x_recv, y_send, y_recv, c_send, c_recv,
):
    d = lax.axis_index("dp")
    y = lax.axis_index("replica")
    z, x, core = d // (NX * NC), (d // NC) % NX, d % NC
    other = 1 - core
    zx = z * NX + x
    mine = zx * NY + y
    partner = device(z, x, other, y)

    def target(k):
        m = (k * 37) % SLOTS
        return (z + m % NZ) % NZ, (x + (m // NZ) % NX) % NX, (y + m // (NZ * NX)) % NY

    def remote(src, dst, send, recv, where):
        return pltpu.make_async_remote_copy(
            src_ref=src, dst_ref=dst, send_sem=send, recv_sem=recv,
            device_id=where, device_id_type=MESH,
        )

    loads = [
        pltpu.make_async_copy(g_hbm, g_ref, in_sem.at[0]),
        pltpu.make_async_copy(a_hbm, a_ref, in_sem.at[1]),
        pltpu.make_async_copy(slot_hbm, slot_row, in_sem.at[3]),
    ]
    for cp in loads[::-1]:
        cp.start()

    along_z = [device((z + k) % NZ, x, core, y) for k in range(1, NZ)]
    along_x = [device(z, (x + k) % NX, core, y) for k in range(1, NX)]
    along_y = [device(z, x, core, (y + k) % NY) for k in range(1, NY)]
    barrier = pltpu.get_barrier_semaphore()

    def greet(sem, devices):
        for one in devices:
            pl.semaphore_signal(sem, inc=1, device_id=one, device_id_type=MESH)

    first = along_z + along_x + along_y + [partner]
    greet(barrier, first)

    loads[2].wait()
    at_slot = lax.broadcasted_iota(jnp.int32, (SLOTS, NBLK), 0) == slot_row[...]
    block = lax.broadcasted_iota(jnp.int32, (SLOTS, NBLK), 1)
    block = jnp.min(jnp.where(at_slot, block, NBLK), axis=1, keepdims=True)
    inv_v[...] = jnp.transpose(jnp.broadcast_to(block, (SLOTS, 128)))[:8]
    to_smem = pltpu.make_async_copy(inv_v, inv_ref, in_sem.at[2])
    to_smem.start()

    pl.semaphore_wait(barrier, len(first))
    greet(meet.at[0], along_y)
    to_smem.wait()
    loads[0].wait()
    pl.semaphore_wait(meet.at[0], len(along_y))
    greet(meet.at[1], along_x)

    half = WIDTH // 2

    def pack(t):
        b = inv_ref[0, t]
        rows = g_ref[jnp.clip(b, 0, NBLK - 1)]
        sbuf[t] = jnp.where(b < NBLK, rows, jnp.zeros_like(rows))

    def send_rows(k):
        tz, tx, ty = target(k)
        t = (tz * NX + tx) * NY + ty
        pack(t)
        remote(
            sbuf.at[t], gbuf.at[y, zx, core], g_send, g_recv.at[y], device(tz, tx, core, ty)
        ).start()

    def is_self(i, q):
        return jnp.logical_and(2 * core + i == y, core == q)

    def send_root(i, q, m, n):
        if m == 0:
            src, dst, recv = rl_ref.at[i, n, q], rlb.at[y * 8 + n], rl_recv
        else:
            rows = pl.ds(pl.multiple_of(q * half + n * (half // 8), half // 8), half // 8)
            src, dst, recv = rr_ref.at[i, rows], rrb.at[y, rows], rr_recv.at[y]

        @pl.when(is_self(i, q))
        def _():
            pltpu.make_async_copy(src, dst, recv).start()

        @pl.when(jnp.logical_not(is_self(i, q)))
        def _():
            remote(src, dst, root_send.at[m, i, q], recv, device(z, x, q, 2 * core + i)).start()

    def first_roots(n, _):
        for i, q in [(i, q) for i in range(2) for q in range(NC)]:
            send_root(i, q, 0, n)
        return 0

    lax.fori_loop(0, 2, first_roots, 0)
    pack(mine)
    own_rows = pltpu.make_async_copy(sbuf.at[mine], gbuf.at[y, zx, core], g_recv.at[y])
    own_rows.start()
    pl.semaphore_wait(meet.at[1], len(along_x))

    def send_some(m, first):
        def some(n, _):
            for u in range(16):
                k = (first + n) * 16 + u

                @pl.when(k > 0)
                def _(k=k):
                    send_rows(k)

                if u % 2 == 1:
                    piece = u // 2

                    @pl.when(k >= 16)
                    def _(piece=piece, n=n):
                        send_root(piece // 2 % 2, piece % 2, m, 2 * n + piece // 4)
            return 0

        return some

    lax.fori_loop(0, 4, send_some(0, 0), 0)
    lax.fori_loop(0, 4, send_some(1, 4), 0)

    gp[...] = jnp.zeros_like(gp)

    def graft(b, _):
        g32 = g_ref[b].astype(F32)
        scaled = g32 / (jnp.sqrt(a_ref[b] + g32 * g32) + 1e-08)
        sq = jnp.sum(scaled * scaled, axis=0, keepdims=True)
        gp[pl.ds(b, 1), :] = sq[:, :128] + sq[:, 128:]
        return 0

    loads[1].wait()
    lax.fori_loop(0, NBLK, graft, 0)
    part = jnp.sum(jnp.transpose(gp[...]), axis=0, keepdims=True)
    def spread(buf, me, count, send, recv, where):
        copies = []
        for k in range(1, count):
            other_one = (me + k) % count
            copies.append(remote(buf.at[me], buf.at[me], send.at[k], recv.at[k], where(other_one)))
        for cp in copies:
            cp.start()
        return copies

    def along(axis, buf, value, count, send, recv):
        me = (z, x, y)[axis]
        buf[me] = value
        return spread(buf, me, count, send, recv, lambda o: device(
            o if axis == 0 else z, o if axis == 1 else x, core, o if axis == 2 else y))

    def finish(copies, buf):
        for cp in copies:
            cp.wait()
        return jnp.sum(buf[...], axis=0)

    x_copies = along(1, ar_x, jnp.broadcast_to(part, (8, 128)), NX, x_send.at[0], x_recv.at[0])
    graft_x = finish(x_copies, ar_x)
    z_copies = along(0, ar_z, graft_x, NZ, z_send.at[0], z_recv.at[0])

    swaps = []
    for c in range(NY):
        drain(gbuf.at[c, :, core], g_recv.at[c])
        cp = remote(gbuf.at[c, :, core], gbuf.at[c, :, core], gx_send.at[c], gx_recv.at[c], partner)
        cp.start()
        swaps.append(cp)
    y_copies = along(2, ar_y, finish(z_copies, ar_z), NY, y_send.at[0], y_recv.at[0])
    for cp in swaps:
        cp.wait_recv()

    owner = y // 2
    i_mine = y % 2

    def left_part(n):
        r = 2 * core + n
        for k in range(NY):
            acc = jnp.zeros((COLS, COLS), F32)
            for c in range(NY):
                acc = acc + lax.dot_general(
                    gbuf[c, pl.ds(r * 8, 8)].reshape(COLS, COLS),
                    gbuf[c, pl.ds((r + k) % NY * 8, 8)].reshape(COLS, COLS),
                    (((1,), (1,)), ((), ())), preferred_element_type=F32,
                )
            lb[n, :, k * COLS:(k + 1) * COLS] = acc.astype(BF16)

    def right_part(n):
        r = 2 * core + n
        for k in range(NY):
            rb[n, :, k * COLS:(k + 1) * COLS] = lax.dot_general(
                gbuf[r].reshape(WIDTH, COLS), gbuf[(r + k) % NY].reshape(WIDTH, COLS),
                (((0,), (0,)), ((), ())), preferred_element_type=F32,
            ).astype(BF16)

    def factor_self(n):
        return jnp.logical_and(2 * core + n == y, core == owner)

    def send_factor(m, n, piece, skip):
        rows = pl.ds(pl.multiple_of(piece * ROWS, ROWS), ROWS)
        columns = pl.ds(skip, WIDTH - skip)
        src = (lb, rb)[m].at[n, rows, columns]
        dst = (left_ref, right_ref)[m].at[i_mine, rows, columns]

        @pl.when(factor_self(n))
        def _():
            pltpu.make_async_copy(src, dst, f_recv.at[m]).start()

        @pl.when(jnp.logical_not(factor_self(n)))
        def _():
            remote(src, dst, f_send.at[m, n], f_recv.at[m], device(z, x, owner, 2 * core + n)).start()

    def send_terms(m):
        def upper(piece, _):
            for n in range(2):
                send_factor(m, n, piece, 0)
            return 0

        def lower(piece, _):
            for n in range(2):
                send_factor(m, n, piece, COLS // 2)
            return 0

        lax.fori_loop(0, ROWS // 2, upper, 0)
        lax.fori_loop(ROWS // 2, ROWS, lower, 0)

    for n in range(2):
        left_part(n)
    send_terms(0)

    drain(rlb, rl_recv)
    rl = rlb[...].reshape(half, WIDTH)
    for c in range(NY):
        hb[:, c * COLS:(c + 1) * COLS] = jnp.dot(
            rl, gbuf[c].reshape(WIDTH, COLS), preferred_element_type=F32
        ).astype(BF16)

    def swap_root(c):
        part = rrb.at[c, pl.ds(pl.multiple_of(core * half, half), half)]
        drain(part, rr_recv.at[c])
        cp = remote(part, part, rx_send.at[c], rx_recv.at[c], partner)
        cp.start()
        return cp

    def send_back(c):
        def one(k, _):
            m = k * 13
            tz, tx = (z + m % NZ) % NZ, (x + (m // NZ) % NX) % NX
            remote(
                sb.at[c, tz * NX + tx], ubr.at[mine], u_send, u_recv, device(tz, tx, core, c)
            ).start()
            return 0

        return one

    sq = jnp.zeros((8, 128), F32)
    quarters = [(y + k) % NY for k in (0, 1, 3, 2)]
    root_swaps = [swap_root(quarters[0])]
    for k, c in enumerate(quarters):
        if k + 1 < NY:
            root_swaps.append(swap_root(quarters[k + 1]))
        root_swaps[k].wait_recv()
        s = jnp.dot(hb[...], rrb[c], preferred_element_type=F32).astype(BF16)
        sb[c] = s.reshape(NZ * NX, ROWS, COLS)
        if k == 0:
            own_dir = pltpu.make_async_copy(sb.at[y, zx], ubr.at[mine], u_recv)
            own_dir.start()
        lax.fori_loop(1 if k == 0 else 0, NZ * NX, send_back(c), 0)
        s32 = s.astype(F32)
        s2 = jnp.sum((s32 * s32).reshape(half // 8, 8, COLS), axis=0)
        sq = sq + s2[:, :128] + s2[:, 128:]

    ar_c[core, 0] = sq
    ar_c[core, 1] = finish(y_copies, ar_y)
    c_copy = remote(ar_c.at[core], ar_c.at[core], c_send, c_recv, partner)
    c_copy.start()
    for n in range(2):
        right_part(n)
    c_copy.wait()
    search_sq = jnp.sum(ar_c[0, 0] + ar_c[1, 0], keepdims=True)
    graft_all = ar_c[0, 1] + ar_c[1, 1]
    lane = lax.broadcasted_iota(jnp.int32, (8, 128), 1)
    graft_sq = jnp.sum(jnp.where(lane[:1] == inv_ref[0, mine], graft_all[:1], 0.0), keepdims=True)
    ratio = jnp.sqrt(graft_sq) / (jnp.sqrt(search_sq) + 1e-06)
    ratio = jnp.where(lane == mine, jnp.broadcast_to(ratio, (8, 128)), 0.0)
    x_ratio = finish(along(1, rt_x, ratio, NX, x_send.at[1], x_recv.at[1]), rt_x)
    y_ratio = along(2, rt_y, x_ratio, NY, y_send.at[1], y_recv.at[1])

    send_terms(1)
    z_ratio = along(0, rt_z, finish(y_ratio, rt_y), NZ, z_send.at[1], z_recv.at[1])
    ratio_ref[...] = finish(z_ratio, rt_z)
    drain(ubr, u_recv)

    drain(sbuf.at[pl.ds(0, 120)], f_recv.at[0])
    drain(sbuf.at[pl.ds(0, 120)], f_recv.at[1])
    drain(sbuf.at[pl.ds(0, SLOTS - 1)], g_send)
    drain(ubr.at[pl.ds(0, SLOTS - 1)], u_send)
    for cp in swaps:
        cp.wait_send()
    for cp in root_swaps:
        cp.wait_send()
    for i in range(2):
        for q in range(NC):
            @pl.when(jnp.logical_not(is_self(i, q)))
            def _(i=i, q=q):
                drain(rlb.at[pl.ds(0, 8)], root_send.at[0, i, q])
                drain(rrb.at[0, pl.ds(0, half)], root_send.at[1, i, q])
    for n in range(2):
        @pl.when(jnp.logical_not(factor_self(n)))
        def _(n=n):
            drain(sbuf.at[pl.ds(0, 60)], f_send.at[0, n])
            drain(sbuf.at[pl.ds(0, 60)], f_send.at[1, n])


def exchange(block_slot, gradients, adagrad, root_left, root_right):
    vmem = pl.BlockSpec(memory_space=pltpu.VMEM)
    hbm = pl.BlockSpec(memory_space=pl.ANY)
    dma = pltpu.SemaphoreType.DMA
    return pl.pallas_call(
        kernel,
        out_shape=(
            pltpu.VMEM((SLOTS, ROWS, COLS), BF16),
            pltpu.VMEM((2, COLS, WIDTH), BF16),
            pltpu.VMEM((2, COLS, WIDTH), BF16),
            jax.ShapeDtypeStruct((8, 128), F32),
        ),
        in_specs=[hbm] * 5,
        out_specs=(hbm, hbm, hbm, vmem),
        scratch_shapes=[
            pltpu.VMEM((NBLK, ROWS, COLS), BF16),
            pltpu.VMEM((NBLK, ROWS, COLS), F32),
            dma((4,)),
            pltpu.SemaphoreType.REGULAR((2,)),
            pltpu.VMEM((1, NBLK), jnp.int32),
            pltpu.VMEM((8, 128), jnp.int32),
            pltpu.SMEM((8, 128), jnp.int32),
            pltpu.VMEM((SLOTS, ROWS, COLS), BF16),
            pltpu.VMEM((NY, NZ * NX, NC, ROWS, COLS), BF16),
            pltpu.VMEM((NZ * NX, ROWS, WIDTH), BF16),
            pltpu.VMEM((NY, WIDTH, COLS), BF16),
            pltpu.VMEM((WIDTH // 2, WIDTH), BF16),
            pltpu.VMEM((NY, NZ * NX, ROWS, COLS), BF16),
            pltpu.VMEM((2, COLS, WIDTH), BF16),
            pltpu.VMEM((2, COLS, WIDTH), BF16),
            pltpu.VMEM((128, 128), F32),
            pltpu.VMEM((NZ, 8, 128), F32),
            pltpu.VMEM((NX, 8, 128), F32),
            pltpu.VMEM((NY, 8, 128), F32),
            pltpu.VMEM((NC, 2, 8, 128), F32),
            pltpu.VMEM((NZ, 8, 128), F32),
            pltpu.VMEM((NX, 8, 128), F32),
            pltpu.VMEM((NY, 8, 128), F32),
            dma, dma((NY,)), dma((NY,)), dma((NY,)), dma((2, 2, NC)), dma, dma((NY,)),
            dma((NY,)), dma((NY,)), dma((2, 2)), dma((2,)), dma, dma,
            dma((2, NZ)), dma((2, NZ)), dma((2, NX)), dma((2, NX)), dma((2, NY)), dma((2, NY)), dma, dma,
        ],
        compiler_params=pltpu.CompilerParams(
            collective_id=0, has_side_effects=True, vmem_limit_bytes=24 * 2**20
        ),
        cost_estimate=pl.CostEstimate(flops=6 * 10**10, bytes_accessed=6 * 2**20, transcendentals=0),
        name="shampoo_exchange",
    )(*(in_hbm(v) for v in (block_slot.reshape(1, NBLK), gradients, adagrad, root_left, root_right)))


def tail_kernel(
    slot, ratio_v, fl, fr, left, right, g, a, directions, fl_out, fr_out, a_out, upd_out,
    f_buf, a_buf, u_buf, ratio, f_sem, a_sem, u_sem, r_sem,
):
    outs = []

    to_smem = pltpu.make_async_copy(ratio_v, ratio, r_sem)
    to_smem.start()
    y = lax.axis_index("replica")
    half = COLS // 2
    for m, (old, term, out) in enumerate(((fl, left, fl_out), (fr, right, fr_out))):
        for n in range(4):
            i, low = n // 2, n % 2
            rows = pl.ds(low * half, half)
            for k in range(NY):
                columns = pl.ds(pl.multiple_of((y + k) % NY * COLS, COLS), COLS)
                if k == 0 and low:
                    mirrored = jnp.transpose(term[i, :half, half:COLS].astype(F32))
                    new = jnp.concatenate([mirrored, term[i, half:, half:COLS].astype(F32)], axis=1)
                else:
                    new = term[i, rows, k * COLS:(k + 1) * COLS].astype(F32)
                f_buf[m, i, rows, columns] = 0.9 * old[i, rows, columns] + 0.1 * new
            outs.append(pltpu.make_async_copy(f_buf.at[m, i, rows], out.at[i, rows], f_sem.at[m, n]))
            outs[-1].start()

    to_smem.wait()

    def scale(b, _):
        t = slot[b]
        u_buf[b] = (directions[t].astype(F32) * ratio[0, t]).astype(BF16)
        return 0

    lax.fori_loop(0, NBLK, scale, 0)
    outs.append(pltpu.make_async_copy(u_buf, upd_out, u_sem))
    outs[-1].start()

    def add(n, _):
        few = pl.ds(n * 4, 4)
        g32 = g[few].astype(F32)
        a_buf[few] = a[few] + g32 * g32
        return 0

    lax.fori_loop(0, NBLK // 4, add, 0)
    outs.append(pltpu.make_async_copy(a_buf, a_out, a_sem))
    outs[-1].start()
    for copy in outs:
        copy.wait()


def tail(block_slot, ratio, factor_left, factor_right, left_term, right_term, gradients, adagrad, directions):
    smem = pl.BlockSpec(memory_space=pltpu.SMEM)
    vmem = pl.BlockSpec(memory_space=pltpu.VMEM)
    hbm = pl.BlockSpec(memory_space=pl.ANY)
    dma = pltpu.SemaphoreType.DMA
    return pl.pallas_call(
        tail_kernel,
        out_shape=(
            jax.ShapeDtypeStruct(factor_left.shape, F32),
            jax.ShapeDtypeStruct(factor_right.shape, F32),
            jax.ShapeDtypeStruct(adagrad.shape, F32),
            jax.ShapeDtypeStruct(gradients.shape, BF16),
        ),
        in_specs=[smem] + [vmem] * 8,
        out_specs=(hbm, hbm, hbm, hbm),
        scratch_shapes=[
            pltpu.VMEM((2, 2, COLS, WIDTH), F32),
            pltpu.VMEM((NBLK, ROWS, COLS), F32),
            pltpu.VMEM((NBLK, ROWS, COLS), BF16),
            pltpu.SMEM((8, 128), F32),
            dma((2, 4)), dma, dma, dma,
        ],
        compiler_params=pltpu.CompilerParams(vmem_limit_bytes=24 * 2**20),
        name="shampoo_tail",
    )(block_slot, ratio, factor_left, factor_right, left_term, right_term, gradients, adagrad, directions)


def on_device(gradients, adagrad, factor_left, factor_right, root_left, root_right, block_slot):
    count = factor_left.shape[0]
    directions, left_term, right_term, ratio = exchange(
        block_slot, gradients, adagrad, root_left.reshape(count, 8, NC, ROWS, WIDTH), root_right
    )
    factor_left_new, factor_right_new, adagrad_new, update = tail(
        block_slot, ratio, factor_left, factor_right, left_term, right_term, gradients, adagrad, directions
    )
    return update, adagrad_new, factor_left_new, factor_right_new


def solution(mesh):
    placed = (
        P(None, "dp", "replica"),
        P(None, "dp", "replica"),
        P("dp", "replica", None),
        P("dp", "replica", None),
        P("dp", "replica", None),
        P("dp", None, "replica"),
        P(),
    )
    return jax.shard_map(
        on_device,
        mesh=mesh,
        in_specs=placed,
        out_specs=(
            P(None, "dp", "replica"),
            P(None, "dp", "replica"),
            P("dp", "replica", None),
            P("dp", "replica", None),
        ),
        check_vma=False,
    )
```
